256 devices in a mesh: sensor: 64 (over y, x, z_lo), tm: 4 (over z_hi, core).
Axes of the slice: x: 4, y: 4, z: 8 (z_hi: 2, z_lo: 4; z = z_hi * 4 + z_lo), core: 2. Of those that a mesh axis runs over, the one named last changes fastest.
Arguments:
- series: bfloat16 [12, 8192, 128], P('tm', 'sensor'), may hold values from -40 to 40
- conv_weight: bfloat16 [3, 128, 256], replicated, may hold values from -0.3125 to 0.3125
- qk_weight: bfloat16 [2, 128, 128], replicated, may hold values from -1 to 1
- value_weight: bfloat16 [128, 128], replicated, may hold values from -0.5 to 0.5
- out_weight: bfloat16 [128, 128], replicated, may hold values from -0.5 to 0.5
- norm_gain: float32 [128], replicated, may hold values from 0.25 to 1.75
Outputs:
- layer_out: bfloat16 [12, 8192, 128], P('tm', 'sensor')
The draws below stay inside these ranges and needn't reach their ends.
All inputs are finite; a program needn't handle non-finite values.
Results may differ from the reference program's by a relative error of at most 0.012.
The reference program's roundings to bfloat16 on the way (of `hidden` and `attended`) count: a program that leaves them out, or rounds other values in their place, can miss the bound.
Values may be sent and summed in bfloat16 or wider, within the bound.
No kernel may reach another device: no remote copies, remote signals or barrier semaphores. Data moves between devices by JAX's collectives and lax.ppermute only.
A program may use at most 64 MiB of HBM per device.

```python
import math
import jax
import jax.numpy as jnp
from jax import lax

D = 128
HEADS = 8
KERNEL = 3
SENSORS = 8192
STEPS = 12


def draw_series(key, part):
    groups = 8
    pieces = jax.random.split(jax.random.fold_in(key, 5), 4)
    patterns = 1.2 * jax.random.truncated_normal(pieces[0], -3.0, 3.0, (groups, D), jnp.float32)
    members = jax.random.randint(pieces[1], (SENSORS,), 0, groups)
    chosen = patterns[members]
    noise_scale = jax.random.uniform(pieces[2], (1, SENSORS, 1), jnp.float32, 0.25, 1.5)
    noise = 0.7 * jax.random.truncated_normal(pieces[3], -4.0, 4.0, (STEPS, SENSORS, D), jnp.float32)
    return (chosen[None, :, :] + noise_scale * noise).astype(jnp.bfloat16)


def draw_qk_weight(key, part):
    pieces = jax.random.split(jax.random.fold_in(key, 11), 2)
    base = jax.random.truncated_normal(pieces[0], -4.0, 4.0, (D, D), jnp.float32) * D ** (-0.5)
    noise = jax.random.truncated_normal(pieces[1], -4.0, 4.0, (D, D), jnp.float32) * D ** (-0.5)
    return jnp.stack([base, 0.8 * base + 0.6 * noise]).astype(jnp.bfloat16)


def centred(rng, extent, deviation, most, held_as=jnp.bfloat16):
    entries = jax.random.normal(rng, extent, jnp.float32) * deviation
    return jnp.minimum(jnp.maximum(entries, -most), most).astype(held_as)


def setup_inputs(seed: int = 0) -> dict:
    arg_keys = jax.random.split(jax.random.key(seed), 7)
    series = draw_series(jax.random.fold_in(arg_keys[6], 71), 0)
    conv_weight = centred(arg_keys[1], (KERNEL, D, 2 * D), (KERNEL * D) ** -0.5, 0.3125)
    qk_weight = draw_qk_weight(jax.random.fold_in(arg_keys[6], 71), 0)
    value_weight = centred(arg_keys[3], (D, D), D ** -0.5, 0.5)
    out_weight = centred(arg_keys[4], (D, D), D ** -0.5, 0.5)
    norm_gain = jnp.clip(1.0 + 0.15 * jax.random.normal(arg_keys[5], (D,), jnp.float32), 0.25, 1.75)
    return dict(series=series, conv_weight=conv_weight, qk_weight=qk_weight, value_weight=value_weight, out_weight=out_weight, norm_gain=norm_gain)


def reference(series, conv_weight, qk_weight, value_weight, out_weight, norm_gain):
    head_dim = D // HEADS
    scale = 1.0 / math.sqrt(head_dim)
    zeros = jnp.zeros((KERNEL - 1, SENSORS, D), series.dtype)
    padded = jnp.concatenate([zeros, series], axis=0)
    conv = jnp.zeros((STEPS * SENSORS, 2 * D), jnp.float32)
    for tap in range(KERNEL):
        window = padded[KERNEL - 1 - tap:KERNEL - 1 - tap + STEPS].reshape(STEPS * SENSORS, D)
        conv = conv + jnp.dot(window, conv_weight[tap], preferred_element_type=jnp.float32)
    flat = series.reshape(STEPS * SENSORS, D).astype(jnp.float32)
    hidden = (flat + conv[:, :D] * jax.nn.sigmoid(conv[:, D:])).astype(jnp.bfloat16)
    query = jnp.dot(hidden, qk_weight[0], preferred_element_type=jnp.float32).astype(jnp.bfloat16)
    keys = jnp.dot(hidden, qk_weight[1], preferred_element_type=jnp.float32).astype(jnp.bfloat16)
    values = jnp.dot(hidden, value_weight, preferred_element_type=jnp.float32).astype(jnp.bfloat16)
    query = query.reshape(STEPS, SENSORS, HEADS, head_dim)
    keys = keys.reshape(STEPS, SENSORS, HEADS, head_dim)
    values = values.reshape(STEPS, SENSORS, HEADS, head_dim)
    block = math.gcd(SENSORS, 512)
    nblocks = SENSORS // block

    def one_step(operands):
        q_step, k_step, v_step = operands
        k_wide = k_step.astype(jnp.float32)
        v_wide = v_step.astype(jnp.float32)

        def one_block(q_block):
            scores = jnp.einsum('bhd,khd->hbk', q_block.astype(jnp.float32), k_wide) * scale
            rowmax = lax.optimization_barrier(jnp.max(scores, axis=-1))
            probs = jnp.exp(scores - rowmax[..., None])
            total = lax.optimization_barrier(jnp.sum(probs, axis=-1))
            weighted = probs.astype(jnp.bfloat16).astype(jnp.float32)
            summed = jnp.einsum('hbk,khd->bhd', weighted, v_wide)
            return summed / jnp.transpose(total)[..., None]
        blocks = lax.map(one_block, q_step.reshape(nblocks, block, HEADS, head_dim))
        return blocks.reshape(SENSORS, HEADS, head_dim)
    attended = lax.map(one_step, (query, keys, values))
    attended = attended.reshape(STEPS * SENSORS, D).astype(jnp.bfloat16)
    mixed = jnp.dot(attended, out_weight, preferred_element_type=jnp.float32) + hidden.astype(jnp.float32)
    mean = lax.optimization_barrier(jnp.mean(mixed, axis=-1, keepdims=True))
    var = lax.optimization_barrier(jnp.mean((mixed - mean) ** 2, axis=-1, keepdims=True))
    normed = (mixed - mean) / jnp.sqrt(var + 1e-05) * norm_gain
    return normed.reshape(STEPS, SENSORS, D).astype(jnp.bfloat16)
```

```python
import functools

import jax
import jax.numpy as jnp
from jax import lax
from jax.experimental import pallas as pl
from jax.experimental.pallas import tpu as pltpu
from jax.sharding import Mesh, PartitionSpec as P

F32 = jnp.float32
BF16 = jnp.bfloat16
HEADS = 8
HEAD_DIM = 16
LOG2E = 1.4426950408889634
AXES = ("y1", "y0", "x1", "x0", "z1", "z0", "zh", "core")
SENSOR = AXES[:6]
TM = AXES[6:]
NEAR = ("y0", "x0", "z0")
FAR = ("y1", "x1", "z1")
VMEM = pl.BlockSpec(memory_space=pltpu.VMEM)
KEYS = 2048
LOWEST = 2.0**-20
HIGHEST = 2.0**100


def split3(x):
    high = x.astype(BF16)
    rest = x - high.astype(F32)
    mid = rest.astype(BF16)
    low = (rest - mid.astype(F32)).astype(BF16)
    return high, mid, low


def first_kernel(earlier, series, conv_w, qk_w, value_w, hidden_ref, qkv_ref):
    steps, sens, width = series.shape
    own = series[...].reshape(steps * sens, width)
    padded = jnp.concatenate([earlier[...].reshape(2 * sens, width), own], axis=0)
    conv = jnp.dot(own, conv_w[0], preferred_element_type=F32)
    for tap in (1, 2):
        window = padded[(2 - tap) * sens : (2 - tap + steps) * sens]
        conv = conv + jnp.dot(window, conv_w[tap], preferred_element_type=F32)
    gate = jax.nn.sigmoid(conv[:, width:])
    hidden = (own.astype(F32) + conv[:, :width] * gate).astype(BF16)
    hidden_ref[...] = hidden
    for part, weight in enumerate((qk_w[0], qk_w[1], value_w[...])):
        rows = jnp.dot(hidden, weight, preferred_element_type=F32).astype(BF16)
        for t in range(steps):
            cols = rows[t * sens : (t + 1) * sens].T
            for h in range(HEADS):
                qkv_ref[h, t, part * HEAD_DIM : (part + 1) * HEAD_DIM, :] = cols[
                    h * HEAD_DIM : (h + 1) * HEAD_DIM
                ]


def attention_kernel(qkv, *refs):
    chunks, out_ref, ka, qa, va, qs = refs[:-5], refs[-5], refs[-4], refs[-3], refs[-2], refs[-1]
    blocks, steps, _, lanes = qkv.shape
    nq = blocks * lanes
    nk = len(chunks) * blocks * lanes
    pairs = blocks // 2
    one = jnp.ones((16, 2 * lanes), BF16)

    def prepare(t):
        for c, chunk in enumerate(chunks):
            for p in range(pairs):
                kv = jnp.concatenate([chunk[2 * p, t], chunk[2 * p + 1, t]], axis=1)
                k = kv[:HEAD_DIM]
                row = (c * pairs + p) * 2 * lanes
                ka[row : row + 2 * lanes, :] = jnp.concatenate([k, k, k, one], axis=0).T
                va[c * pairs + p] = jnp.concatenate([kv[HEAD_DIM:], one], axis=0)
        for b in range(blocks):
            q = qkv[b, t, :HEAD_DIM, :]
            qs[:, b * lanes : (b + 1) * lanes] = q
            parts = split3(q.astype(F32) * (0.25 * LOG2E))
            qa[:48, b * lanes : (b + 1) * lanes] = jnp.concatenate(parts, axis=0)

    def store(t, value):
        for b in range(blocks):
            out_ref[b, t] = value[:, b * lanes : (b + 1) * lanes].astype(BF16)

    def fast(t, bad):
        prepare(t)
        sample = jnp.dot(ka[:256, :48], qa[:48, :], preferred_element_type=F32)
        shift = split3(-jnp.max(sample, axis=0, keepdims=True))
        row = lax.broadcasted_iota(jnp.int32, (16, nq), 0)
        rows = jnp.zeros((16, nq), F32)
        for i, part in enumerate(shift):
            rows = jnp.where(row == i, part.astype(F32), rows)
        qa[48:, :] = rows.astype(BF16)
        qq = qa[...]

        def block(i, acc):
            off = pl.multiple_of(i * KEYS, KEYS)
            s = jnp.dot(ka[pl.ds(off, KEYS), :], qq, preferred_element_type=F32)
            p = jnp.exp2(s).astype(BF16)
            for u in range(KEYS // 256):
                acc = acc + jnp.dot(
                    va[i * (KEYS // 256) + u],
                    p[u * 256 : (u + 1) * 256],
                    preferred_element_type=F32,
                )
            return acc

        acc = lax.fori_loop(0, nk // KEYS, block, jnp.zeros((32, nq), F32))
        total = acc[HEAD_DIM : HEAD_DIM + 1]
        store(t, acc[:HEAD_DIM] / total)
        good = (total >= LOWEST) & (total <= HIGHEST)
        return jnp.maximum(bad, jnp.where(good, 0.0, 1.0))

    bad = lax.fori_loop(0, steps, fast, jnp.zeros((1, nq), F32))

    @pl.when(jnp.max(bad) > 0.0)
    def exact():
        def step(t, carry):
            prepare(t)
            qq = qs[...]

            def scores(i):
                off = pl.multiple_of(i * 256, 256)
                k = ka[pl.ds(off, 256), :HEAD_DIM]
                return jnp.dot(k, qq, preferred_element_type=F32) * 0.25

            def largest(i, top):
                return jnp.maximum(top, jnp.max(scores(i), axis=0, keepdims=True))

            top = lax.fori_loop(0, nk // 256, largest, jnp.full((1, nq), -jnp.inf, F32))

            def block(i, acc):
                p = jnp.exp(scores(i) - top).astype(BF16)
                return acc + jnp.dot(va[i], p, preferred_element_type=F32)

            acc = lax.fori_loop(0, nk // 256, block, jnp.zeros((32, nq), F32))
            store(t, acc[:HEAD_DIM] / acc[HEAD_DIM : HEAD_DIM + 1])
            return carry

        lax.fori_loop(0, steps, step, 0)


def last_kernel(attended, hidden, out_w, gain, out_ref):
    heads, steps, dim, sens = attended.shape
    width = heads * dim
    for t in range(steps):
        rows = attended[:, t].reshape(width, sens).T
        mixed = jnp.dot(rows, out_w[...], preferred_element_type=F32)
        mixed = mixed + hidden[t * sens : (t + 1) * sens, :].astype(F32)
        mean = jnp.mean(mixed, axis=-1, keepdims=True)
        centred = mixed - mean
        var = jnp.mean(centred * centred, axis=-1, keepdims=True)
        out_ref[t] = (centred / jnp.sqrt(var + 1e-5) * gain[...]).astype(BF16)


def local(series, conv_weight, qk_weight, value_weight, out_weight, norm_gain):
    steps, sens, width = series.shape
    blocks = lax.axis_size(TM)
    earlier = lax.ppermute(series[steps - 2 :], TM, [(i, i + 1) for i in range(blocks - 1)])
    hidden, qkv = pl.pallas_call(
        first_kernel,
        out_shape=(
            jax.ShapeDtypeStruct((steps * sens, width), BF16),
            jax.ShapeDtypeStruct((HEADS, steps, 3 * HEAD_DIM, sens), BF16),
        ),
        in_specs=[VMEM] * 5,
        out_specs=(VMEM, VMEM),
        compiler_params=pltpu.CompilerParams(vmem_limit_bytes=32 << 20),
    )(earlier, series, conv_weight, qk_weight, value_weight)
    qkv = lax.all_to_all(qkv, NEAR, 0, 0, tiled=True)
    kv = qkv[:, :, HEAD_DIM:, :]
    groups = lax.axis_size(FAR)
    chunks = [kv]
    for mask in range(1, groups):
        chunks.append(lax.ppermute(kv, FAR, [(i, i ^ mask) for i in range(groups)]))
    near = qkv.shape[0]
    nq, nk = near * sens, groups * near * sens
    attended = pl.pallas_call(
        attention_kernel,
        out_shape=jax.ShapeDtypeStruct((near, steps, HEAD_DIM, sens), BF16),
        in_specs=[VMEM] * (1 + groups),
        out_specs=VMEM,
        scratch_shapes=[
            pltpu.VMEM((nk, 64), BF16),
            pltpu.VMEM((64, nq), BF16),
            pltpu.VMEM((nk // 256, 32, 256), BF16),
            pltpu.VMEM((HEAD_DIM, nq), BF16),
        ],
        compiler_params=pltpu.CompilerParams(vmem_limit_bytes=48 << 20),
    )(qkv, *chunks)
    attended = lax.all_to_all(attended, NEAR, 0, 0, tiled=True)
    return pl.pallas_call(
        last_kernel,
        out_shape=jax.ShapeDtypeStruct((steps, sens, width), BF16),
        in_specs=[VMEM] * 4,
        out_specs=VMEM,
        compiler_params=pltpu.CompilerParams(vmem_limit_bytes=32 << 20),
    )(attended, hidden, out_weight, norm_gain.reshape(1, width))


def solution(mesh):
    fine = Mesh(mesh.devices.reshape((2,) * len(AXES)), AXES)
    spec = P(TM, SENSOR, None)
    return jax.shard_map(
        local,
        mesh=fine,
        in_specs=(spec, P(), P(), P(), P(), P()),
        out_specs=spec,
        check_vma=False,
    )
```

```python
import functools

import jax
import jax.numpy as jnp
from jax import lax
from jax.experimental import pallas as pl
from jax.experimental.pallas import tpu as pltpu
from jax.sharding import Mesh, PartitionSpec as P

F32 = jnp.float32
BF16 = jnp.bfloat16
HEADS = 8
HEAD_DIM = 16
LOG2E = 1.4426950408889634
AXES = ("y1", "y0", "x1", "x0", "z1", "z0", "zh", "core")
SENSOR = AXES[:6]
TM = AXES[6:]
NEAR = ("y0", "x0", "z0")
VMEM = pl.BlockSpec(memory_space=pltpu.VMEM)
SMEM = pl.BlockSpec(memory_space=pltpu.SMEM)
LOWEST = 2.0**-20
HIGHEST = 2.0**100


def split3(x):
    high = x.astype(BF16)
    rest = x - high.astype(F32)
    mid = rest.astype(BF16)
    low = (rest - mid.astype(F32)).astype(BF16)
    return high, mid, low


def first_kernel(mirror, earlier, series, conv_w, qk_w, value_w, hidden_ref, qkv_ref):
    flip = mirror[0]
    steps, sens, width = series.shape
    own = series[...].reshape(steps * sens, width)
    padded = jnp.concatenate([earlier[...].reshape(2 * sens, width), own], axis=0)
    conv = jnp.dot(own, conv_w[0], preferred_element_type=F32)
    for tap in (1, 2):
        window = padded[(2 - tap) * sens : (2 - tap + steps) * sens]
        conv = conv + jnp.dot(window, conv_w[tap], preferred_element_type=F32)
    gate = jax.nn.sigmoid(conv[:, width:])
    hidden = (own.astype(F32) + conv[:, :width] * gate).astype(BF16)
    hidden_ref[...] = hidden
    for part, weight in enumerate((qk_w[0], qk_w[1], value_w[...])):
        rows = jnp.dot(hidden, weight, preferred_element_type=F32).astype(BF16)
        for t in range(steps):
            cols = rows[t * sens : (t + 1) * sens].T
            for h in range(HEADS):
                qkv_ref[h ^ flip, t, part * HEAD_DIM : (part + 1) * HEAD_DIM, :] = cols[
                    h * HEAD_DIM : (h + 1) * HEAD_DIM
                ]


def absorb(t, qq, acc, chunks, ka, va):
    blocks, lanes = chunks[0].shape[0], chunks[0].shape[3]
    one = jnp.ones((16, 2 * lanes), BF16)
    for c, chunk in enumerate(chunks):
        for p in range(blocks // 2):
            kv = jnp.concatenate([chunk[2 * p, t, -32:], chunk[2 * p + 1, t, -32:]], axis=1)
            k = kv[:HEAD_DIM]
            pair = c * (blocks // 2) + p
            ka[pair * 256 : (pair + 1) * 256, :] = jnp.concatenate([k, k, k, one], axis=0).T
            va[pair] = jnp.concatenate([kv[HEAD_DIM:], one], axis=0)
    pairs = len(chunks) * (blocks // 2)
    s = jnp.dot(ka[: pairs * 256, :], qq, preferred_element_type=F32)
    p = jnp.exp2(s).astype(BF16)
    for u in range(pairs):
        acc = acc + jnp.dot(va[u], p[u * 256 : (u + 1) * 256], preferred_element_type=F32)
    return acc


def begin_kernel(qkv, qa_ref, acc_ref, ka, va):
    blocks, steps, _, lanes = qkv.shape
    nq = blocks * lanes

    def step(t, carry):
        qa = qa_ref.at[t]
        for b in range(blocks):
            parts = split3(qkv[b, t, :HEAD_DIM, :].astype(F32) * (0.25 * LOG2E))
            qa[:48, b * lanes : (b + 1) * lanes] = jnp.concatenate(parts, axis=0)
        k = jnp.concatenate([qkv[0, t, HEAD_DIM:32, :], qkv[1, t, HEAD_DIM:32, :]], axis=1)
        k = jnp.concatenate([k, k, k], axis=0).T
        sample = jnp.dot(k, qa[:48, :], preferred_element_type=F32)
        shift = split3(-jnp.max(sample, axis=0, keepdims=True))
        row = lax.broadcasted_iota(jnp.int32, (16, nq), 0)
        rows = jnp.zeros((16, nq), F32)
        for i, part in enumerate(shift):
            rows = jnp.where(row == i, part.astype(F32), rows)
        qa[48:, :] = rows.astype(BF16)
        acc_ref[t] = absorb(t, qa[...], jnp.zeros((32, nq), F32), [qkv], ka, va)
        return carry

    lax.fori_loop(0, steps, step, 0)


def more_kernel(qa, acc_in, *refs):
    chunks, acc_out, ka, va = refs[:-3], refs[-3], refs[-2], refs[-1]

    def step(t, carry):
        acc_out[t] = absorb(t, qa[t], acc_in[t], chunks, ka, va)
        return carry

    lax.fori_loop(0, qa.shape[0], step, 0)


def end_kernel(count, qa, acc_in, qkv, *refs):
    chunks, out_ref, ka, va = refs[:-3], refs[-3], refs[-2], refs[-1]
    late = chunks[len(chunks) - count :]
    blocks, steps, _, lanes = qkv.shape
    nq = blocks * lanes

    def store(t, value):
        for b in range(blocks):
            out_ref[b, t] = value[:, b * lanes : (b + 1) * lanes].astype(BF16)

    def fast(t, bad):
        acc = absorb(t, qa[t], acc_in[t], late, ka, va)
        total = acc[HEAD_DIM : HEAD_DIM + 1]
        store(t, acc[:HEAD_DIM] / total)
        good = (total >= LOWEST) & (total <= HIGHEST)
        return jnp.maximum(bad, jnp.where(good, 0.0, 1.0))

    bad = lax.fori_loop(0, steps, fast, jnp.zeros((1, nq), F32))

    @pl.when(jnp.max(bad) > 0.0)
    def exact():
        one = jnp.ones((16, lanes), BF16)

        def step(t, carry):
            qq = jnp.concatenate([qkv[b, t, :HEAD_DIM, :] for b in range(blocks)], axis=1)

            def scores(chunk, i):
                k = chunk[i, t, -32:-HEAD_DIM].T
                return jnp.dot(k, qq, preferred_element_type=F32) * 0.25

            top = jnp.full((1, nq), -jnp.inf, F32)
            for chunk in (qkv, *chunks):

                def largest(i, top):
                    return jnp.maximum(top, jnp.max(scores(chunk, i), axis=0, keepdims=True))

                top = lax.fori_loop(0, blocks, largest, top)
            acc = jnp.zeros((32, nq), F32)
            for chunk in (qkv, *chunks):

                def block(i, acc):
                    p = jnp.exp(scores(chunk, i) - top).astype(BF16)
                    v = jnp.concatenate([chunk[i, t, -HEAD_DIM:], one], axis=0)
                    return acc + jnp.dot(v, p, preferred_element_type=F32)

                acc = lax.fori_loop(0, blocks, block, acc)
            store(t, acc[:HEAD_DIM] / acc[HEAD_DIM : HEAD_DIM + 1])
            return carry

        lax.fori_loop(0, steps, step, 0)


def attention(kernel, operands, out_shape, chunks, aliases={}):
    shape = operands[-1].shape
    near, steps, _, sens = shape
    keys = chunks * near * sens
    return pl.pallas_call(
        kernel,
        out_shape=out_shape,
        in_specs=[VMEM] * len(operands),
        out_specs=jax.tree.map(lambda _: VMEM, out_shape),
        scratch_shapes=[
            pltpu.VMEM((keys, 64), BF16),
            pltpu.VMEM((keys // 256, 32, 256), BF16),
        ],
        input_output_aliases=aliases,
        cost_estimate=pl.CostEstimate(
            flops=2 * keys * near * sens * steps * 256 * 2,
            bytes_accessed=0,
            transcendentals=keys * near * sens * steps,
        ),
        compiler_params=pltpu.CompilerParams(vmem_limit_bytes=48 << 20),
    )(*operands)


def last_kernel(mirror, attended, hidden, out_w, gain, out_ref):
    flip = mirror[0]
    heads, steps, dim, sens = attended.shape
    width = heads * dim
    for t in range(steps):
        rows = jnp.concatenate([attended[h ^ flip, t] for h in range(heads)], axis=0).T
        mixed = jnp.dot(rows, out_w[...], preferred_element_type=F32)
        mixed = mixed + hidden[t * sens : (t + 1) * sens, :].astype(F32)
        mean = jnp.mean(mixed, axis=-1, keepdims=True)
        centred = mixed - mean
        var = jnp.mean(centred * centred, axis=-1, keepdims=True)
        out_ref[t] = (centred / jnp.sqrt(var + 1e-5) * gain[...]).astype(BF16)


def local(series, conv_weight, qk_weight, value_weight, out_weight, norm_gain):
    steps, sens, width = series.shape
    blocks = lax.axis_size(TM)
    mirror = (lax.axis_index("y1") * 4 + lax.axis_index("x1") * 2).astype(jnp.int32).reshape(1)
    earlier = lax.ppermute(series[steps - 2 :], TM, [(i, i + 1) for i in range(blocks - 1)])
    hidden, qkv = pl.pallas_call(
        first_kernel,
        out_shape=(
            jax.ShapeDtypeStruct((steps * sens, width), BF16),
            jax.ShapeDtypeStruct((HEADS, steps, 3 * HEAD_DIM, sens), BF16),
        ),
        in_specs=[SMEM] + [VMEM] * 5,
        out_specs=(VMEM, VMEM),
        compiler_params=pltpu.CompilerParams(vmem_limit_bytes=32 << 20),
    )(mirror, earlier, series, conv_weight, qk_weight, value_weight)
    qkv = lax.all_to_all(qkv, NEAR, 0, 0, tiled=True)
    kv = qkv[:, :, HEAD_DIM:, :]

    def swap(block, mask):
        return lax.ppermute(block, SENSOR, [(i, i ^ mask) for i in range(64)])

    along_z, along_y, along_x = 0b000010, 0b110000, 0b001100
    from_z = swap(kv, along_z)
    from_y = swap(kv, along_y)
    from_x = swap(kv, along_x)
    from_xy = swap(kv, along_x | along_y)
    later = [swap(from_z, m) for m in (along_y, along_x, along_x | along_y)]
    near = qkv.shape[0]
    nq = near * sens
    state = (
        jax.ShapeDtypeStruct((steps, 64, nq), BF16),
        jax.ShapeDtypeStruct((steps, 32, nq), F32),
    )
    qa, acc = attention(begin_kernel, (qkv,), state, 1)
    acc = attention(more_kernel, (qa, acc, from_z, from_y), state[1], 2, {1: 0})
    acc = attention(more_kernel, (qa, acc, from_x, from_xy), state[1], 2, {1: 0})
    attended = attention(
        functools.partial(end_kernel, 3),
        (qa, acc, qkv, from_z, from_y, from_x, from_xy, *later),
        jax.ShapeDtypeStruct((near, steps, HEAD_DIM, sens), BF16),
        3,
    )
    attended = lax.all_to_all(attended, NEAR, 0, 0, tiled=True)
    return pl.pallas_call(
        last_kernel,
        out_shape=jax.ShapeDtypeStruct((steps, sens, width), BF16),
        in_specs=[SMEM] + [VMEM] * 4,
        out_specs=VMEM,
        compiler_params=pltpu.CompilerParams(vmem_limit_bytes=32 << 20),
    )(mirror, attended, hidden, out_weight, norm_gain.reshape(1, width))


def solution(mesh):
    fine = Mesh(mesh.devices.reshape((2,) * len(AXES)), AXES)
    spec = P(TM, SENSOR, None)
    return jax.shard_map(
        local,
        mesh=fine,
        in_specs=(spec, P(), P(), P(), P(), P()),
        out_specs=spec,
        check_vma=False,
    )
```

```python
import functools

import jax
import jax.numpy as jnp
from jax import lax
from jax.experimental import pallas as pl
from jax.experimental.pallas import tpu as pltpu
from jax.sharding import Mesh, PartitionSpec as P

F32 = jnp.float32
BF16 = jnp.bfloat16
HEADS = 8
HEAD_DIM = 16
LOG2E = 1.4426950408889634
AXES = ("y1", "y0", "x1", "x0", "z1", "z0", "zh", "core")
SENSOR = AXES[:6]
TM = AXES[6:]
NEAR = ("y0", "x0", "z0")
VMEM = pl.BlockSpec(memory_space=pltpu.VMEM)
SMEM = pl.BlockSpec(memory_space=pltpu.SMEM)
TILE = 512
LOWEST = 2.0**-20
HIGHEST = 2.0**100


def split3(x):
    high = x.astype(BF16)
    rest = x - high.astype(F32)
    mid = rest.astype(BF16)
    low = (rest - mid.astype(F32)).astype(BF16)
    return high, mid, low


def early_kernel(series, conv_w, gain, conv_ref, gain_ref):
    steps, sens, width = series.shape
    own = series[...].reshape(steps * sens, width)
    conv_ref[...] = jnp.dot(own, conv_w[0], preferred_element_type=F32)
    for tap in (1, 2):
        rows = (steps - tap) * sens
        conv_ref[tap * sens :, :] += jnp.dot(own[:rows], conv_w[tap], preferred_element_type=F32)
    gain_ref[...] = gain[...]


def first_kernel(mirror, earlier, series, conv_own, conv_w, qk_w, value_w, hidden_ref, qkv_ref):
    flip = mirror[0]
    steps, sens, width = series.shape
    own = series[...].reshape(steps * sens, width)
    before = earlier[steps - 2 :].reshape(2 * sens, width)
    late = jnp.dot(before, conv_w[2], preferred_element_type=F32)
    near = jnp.dot(before[sens:], conv_w[1], preferred_element_type=F32)
    late = late + jnp.concatenate([near, jnp.zeros_like(near)], axis=0)
    conv = conv_own[...]
    conv = jnp.concatenate([conv[: 2 * sens] + late, conv[2 * sens :]], axis=0)
    gate = jax.nn.sigmoid(conv[:, width:])
    hidden = (own.astype(F32) + conv[:, :width] * gate).astype(BF16)
    hidden_ref[...] = hidden
    for part, weight in enumerate((qk_w[0], qk_w[1], value_w[...])):
        rows = jnp.dot(hidden, weight, preferred_element_type=F32).astype(BF16)
        for t in range(steps):
            cols = rows[t * sens : (t + 1) * sens].T
            for h in range(HEADS):
                qkv_ref[h ^ flip, t, part * HEAD_DIM : (part + 1) * HEAD_DIM, :] = cols[
                    h * HEAD_DIM : (h + 1) * HEAD_DIM
                ]


def absorb(t, qq, acc, chunks, ka, va):
    blocks, lanes = chunks[0].shape[0], chunks[0].shape[3]
    one = jnp.ones((16, 2 * lanes), BF16)
    for c, chunk in enumerate(chunks):
        for p in range(blocks // 2):
            kv = jnp.concatenate([chunk[2 * p, t, -32:], chunk[2 * p + 1, t, -32:]], axis=1)
            k = kv[:HEAD_DIM]
            pair = c * (blocks // 2) + p
            ka[pair * 256 : (pair + 1) * 256, :] = jnp.concatenate([k, k, k, one], axis=0).T
            va[pair] = jnp.concatenate([kv[HEAD_DIM:], one], axis=0)
    pairs = len(chunks) * (blocks // 2)
    sums = []
    for start in range(0, acc.shape[1], TILE):
        cut = slice(start, start + TILE)
        s = jnp.dot(ka[: pairs * 256, :], qq[:, cut], preferred_element_type=F32)
        p = jnp.exp2(s).astype(BF16)
        part = acc[:, cut]
        for u in range(pairs):
            part = part + jnp.dot(va[u], p[u * 256 : (u + 1) * 256], preferred_element_type=F32)
        sums.append(part)
    return jnp.concatenate(sums, axis=1)


def begin_kernel(qkv, qa_ref, acc_ref, ka, va):
    blocks, steps, _, lanes = qkv.shape
    nq = blocks * lanes

    for t in range(steps):
        qa = qa_ref.at[t]
        for b in range(blocks):
            parts = split3(qkv[b, t, :HEAD_DIM, :].astype(F32) * (0.25 * LOG2E))
            qa[:48, b * lanes : (b + 1) * lanes] = jnp.concatenate(parts, axis=0)
        k = jnp.concatenate([qkv[0, t, HEAD_DIM:32, :], qkv[1, t, HEAD_DIM:32, :]], axis=1)
        k = jnp.concatenate([k, k, k], axis=0).T
        sample = jnp.dot(k, qa[:48, :], preferred_element_type=F32)
        shift = split3(-jnp.max(sample, axis=0, keepdims=True))
        row = lax.broadcasted_iota(jnp.int32, (16, nq), 0)
        rows = jnp.zeros((16, nq), F32)
        for i, part in enumerate(shift):
            rows = jnp.where(row == i, part.astype(F32), rows)
        qa[48:, :] = rows.astype(BF16)
        acc_ref[t] = absorb(t, qa[...], jnp.zeros((32, nq), F32), [qkv], ka.at[t], va.at[t])


def more_kernel(qa, acc_in, *refs):
    chunks, acc_out, ka, va = refs[:-3], refs[-3], refs[-2], refs[-1]

    for t in range(qa.shape[0]):
        acc_out[t] = absorb(t, qa[t], acc_in[t], chunks, ka.at[t], va.at[t])


def end_kernel(count, qa, acc_in, qkv, *refs):
    chunks, out_ref, ka, va = refs[:-3], refs[-3], refs[-2], refs[-1]
    late = chunks[len(chunks) - count :]
    blocks, steps, _, lanes = qkv.shape
    nq = blocks * lanes

    def store(t, value):
        for b in range(blocks):
            out_ref[b, t] = value[:, b * lanes : (b + 1) * lanes].astype(BF16)

    bad = jnp.zeros((1, nq), F32)
    for t in range(steps):
        acc = absorb(t, qa[t], acc_in[t], late, ka.at[t], va.at[t])
        total = acc[HEAD_DIM : HEAD_DIM + 1]
        store(t, acc[:HEAD_DIM] / total)
        good = (total >= LOWEST) & (total <= HIGHEST)
        bad = jnp.maximum(bad, jnp.where(good, 0.0, 1.0))

    @pl.when(jnp.max(bad) > 0.0)
    def exact():
        one = jnp.ones((16, lanes), BF16)

        def step(t, carry):
            qq = jnp.concatenate([qkv[b, t, :HEAD_DIM, :] for b in range(blocks)], axis=1)

            def scores(chunk, i):
                k = chunk[i, t, -32:-HEAD_DIM].T
                return jnp.dot(k, qq, preferred_element_type=F32) * 0.25

            top = jnp.full((1, nq), -jnp.inf, F32)
            for chunk in (qkv, *chunks):

                def largest(i, top):
                    return jnp.maximum(top, jnp.max(scores(chunk, i), axis=0, keepdims=True))

                top = lax.fori_loop(0, blocks, largest, top)
            acc = jnp.zeros((32, nq), F32)
            for chunk in (qkv, *chunks):

                def block(i, acc):
                    p = jnp.exp(scores(chunk, i) - top).astype(BF16)
                    v = jnp.concatenate([chunk[i, t, -HEAD_DIM:], one], axis=0)
                    return acc + jnp.dot(v, p, preferred_element_type=F32)

                acc = lax.fori_loop(0, blocks, block, acc)
            store(t, acc[:HEAD_DIM] / acc[HEAD_DIM : HEAD_DIM + 1])
            return carry

        lax.fori_loop(0, steps, step, 0)


def attention(kernel, operands, out_shape, chunks, aliases={}):
    shape = operands[-1].shape
    near, steps, _, sens = shape
    keys = chunks * near * sens
    return pl.pallas_call(
        kernel,
        out_shape=out_shape,
        in_specs=[VMEM] * len(operands),
        out_specs=jax.tree.map(lambda _: VMEM, out_shape),
        scratch_shapes=[
            pltpu.VMEM((steps, keys, 64), BF16),
            pltpu.VMEM((steps, keys // 256, 32, 256), BF16),
        ],
        input_output_aliases=aliases,
        cost_estimate=pl.CostEstimate(
            flops=2 * keys * near * sens * steps * 256 * 2,
            bytes_accessed=0,
            transcendentals=keys * near * sens * steps,
        ),
        compiler_params=pltpu.CompilerParams(vmem_limit_bytes=48 << 20),
    )(*operands)


def last_kernel(mirror, attended, hidden, out_w, gain, out_ref):
    flip = mirror[0]
    heads, steps, dim, sens = attended.shape
    width = heads * dim
    for t in range(steps):
        rows = jnp.concatenate([attended[h ^ flip, t] for h in range(heads)], axis=0).T
        mixed = jnp.dot(rows, out_w[...], preferred_element_type=F32)
        mixed = mixed + hidden[t * sens : (t + 1) * sens, :].astype(F32)
        mean = jnp.mean(mixed, axis=-1, keepdims=True)
        centred = mixed - mean
        var = jnp.mean(centred * centred, axis=-1, keepdims=True)
        out_ref[t] = (centred / jnp.sqrt(var + 1e-5) * gain[...]).astype(BF16)


def local(series, conv_weight, qk_weight, value_weight, out_weight, norm_gain):
    steps, sens, width = series.shape
    blocks = lax.axis_size(TM)
    mirror = (lax.axis_index("y1") * 4 + lax.axis_index("x1") * 2).astype(jnp.int32).reshape(1)
    earlier = lax.ppermute(series, TM, [(i, i + 1) for i in range(blocks - 1)])
    conv_own, gain = pl.pallas_call(
        early_kernel,
        out_shape=(
            jax.ShapeDtypeStruct((steps * sens, 2 * width), F32),
            jax.ShapeDtypeStruct((1, width), F32),
        ),
        in_specs=[VMEM] * 3,
        out_specs=(VMEM, VMEM),
        cost_estimate=pl.CostEstimate(
            flops=2 * 3 * steps * sens * width * 2 * width, bytes_accessed=0, transcendentals=0
        ),
        compiler_params=pltpu.CompilerParams(vmem_limit_bytes=32 << 20),
    )(series, conv_weight, norm_gain.reshape(1, width))
    hidden, qkv = pl.pallas_call(
        first_kernel,
        out_shape=(
            jax.ShapeDtypeStruct((steps * sens, width), BF16),
            jax.ShapeDtypeStruct((HEADS, steps, 3 * HEAD_DIM, sens), BF16),
        ),
        in_specs=[SMEM] + [VMEM] * 6,
        out_specs=(VMEM, VMEM),
        compiler_params=pltpu.CompilerParams(vmem_limit_bytes=32 << 20),
    )(mirror, earlier, series, conv_own, conv_weight, qk_weight, value_weight)
    qkv = lax.all_to_all(qkv, NEAR, 0, 0, tiled=True)
    kv = qkv[:, :, HEAD_DIM:, :]

    def swap(block, mask):
        return lax.ppermute(block, SENSOR, [(i, i ^ mask) for i in range(64)])

    along_z, along_y, along_x = 0b000010, 0b110000, 0b001100
    from_z = swap(kv, along_z)
    from_y = swap(kv, along_y)
    from_x = swap(kv, along_x)
    from_xy = swap(kv, along_x | along_y)
    later = [swap(from_z, m) for m in (along_y, along_x, along_x | along_y)]
    near = qkv.shape[0]
    nq = near * sens
    state = (
        jax.ShapeDtypeStruct((steps, 64, nq), BF16),
        jax.ShapeDtypeStruct((steps, 32, nq), F32),
    )
    qa, acc = attention(begin_kernel, (qkv,), state, 1)
    acc = attention(more_kernel, (qa, acc, from_z, from_y), state[1], 2, {1: 0})
    acc = attention(more_kernel, (qa, acc, from_x, from_xy), state[1], 2, {1: 0})
    attended = attention(
        functools.partial(end_kernel, 3),
        (qa, acc, qkv, from_z, from_y, from_x, from_xy, *later),
        jax.ShapeDtypeStruct((near, steps, HEAD_DIM, sens), BF16),
        3,
    )
    attended = lax.all_to_all(attended, NEAR, 0, 0, tiled=True)
    return pl.pallas_call(
        last_kernel,
        out_shape=jax.ShapeDtypeStruct((steps, sens, width), BF16),
        in_specs=[SMEM] + [VMEM] * 4,
        out_specs=VMEM,
        compiler_params=pltpu.CompilerParams(vmem_limit_bytes=32 << 20),
    )(mirror, attended, hidden, out_weight, gain)


def solution(mesh):
    fine = Mesh(mesh.devices.reshape((2,) * len(AXES)), AXES)
    spec = P(TM, SENSOR, None)
    return jax.shard_map(
        local,
        mesh=fine,
        in_specs=(spec, P(), P(), P(), P(), P()),
        out_specs=spec,
        check_vma=False,
    )
```

```python
import functools

import jax
import jax.numpy as jnp
from jax import lax
from jax.experimental import pallas as pl
from jax.experimental.pallas import tpu as pltpu
from jax.sharding import Mesh, PartitionSpec as P

F32 = jnp.float32
BF16 = jnp.bfloat16
HEADS = 8
HEAD_DIM = 16
LOG2E = 1.4426950408889634
AXES = ("y1", "y0", "x1", "x0", "z1", "z0", "zh", "core")
SENSOR = AXES[:6]
TM = AXES[6:]
NEAR = ("y0", "x0", "z0")
VMEM = pl.BlockSpec(memory_space=pltpu.VMEM)
SMEM = pl.BlockSpec(memory_space=pltpu.SMEM)
TILE = 512
ROWS = HEAD_DIM + 8
LOWEST = 2.0**-20
HIGHEST = 2.0**100


def split3(x):
    high = x.astype(BF16)
    rest = x - high.astype(F32)
    mid = rest.astype(BF16)
    low = (rest - mid.astype(F32)).astype(BF16)
    return high, mid, low


def early_kernel(series, conv_w, gain, conv_ref, gain_ref):
    steps, sens, width = series.shape
    own = series[...].reshape(steps * sens, width)
    conv_ref[...] = jnp.dot(own, conv_w[0], preferred_element_type=F32)
    for tap in (1, 2):
        rows = (steps - tap) * sens
        conv_ref[tap * sens :, :] += jnp.dot(own[:rows], conv_w[tap], preferred_element_type=F32)
    gain_ref[...] = gain[...]


def first_kernel(mirror, earlier, series, conv_own, conv_w, qk_w, value_w, hidden_ref, qkv_ref):
    flip = mirror[0]
    steps, sens, width = series.shape
    own = series[...].reshape(steps * sens, width)
    before = earlier[...].reshape(2 * sens, width)
    late = jnp.dot(before, conv_w[2], preferred_element_type=F32)
    near = jnp.dot(before[sens:], conv_w[1], preferred_element_type=F32)
    late = late + jnp.concatenate([near, jnp.zeros_like(near)], axis=0)
    conv = conv_own[...]
    conv = jnp.concatenate([conv[: 2 * sens] + late, conv[2 * sens :]], axis=0)
    gate = jax.nn.sigmoid(conv[:, width:])
    hidden = (own.astype(F32) + conv[:, :width] * gate).astype(BF16)
    hidden_ref[...] = hidden
    for part, weight in enumerate((qk_w[0], qk_w[1], value_w[...])):
        rows = jnp.dot(hidden, weight, preferred_element_type=F32).astype(BF16)
        for t in range(steps):
            cols = rows[t * sens : (t + 1) * sens].T
            for h in range(HEADS):
                qkv_ref[h ^ flip, t, part * HEAD_DIM : (part + 1) * HEAD_DIM, :] = cols[
                    h * HEAD_DIM : (h + 1) * HEAD_DIM
                ]


def absorb(t, qq, acc, chunks, ka, va):
    blocks, lanes = chunks[0].shape[0], chunks[0].shape[3]
    one = jnp.ones((16, 2 * lanes), BF16)
    for c, chunk in enumerate(chunks):
        for p in range(blocks // 2):
            kv = jnp.concatenate([chunk[2 * p, t, -32:], chunk[2 * p + 1, t, -32:]], axis=1)
            k = kv[:HEAD_DIM]
            pair = c * (blocks // 2) + p
            ka[pair * 256 : (pair + 1) * 256, :] = jnp.concatenate([k, k, k, one], axis=0).T
            va[pair] = kv[HEAD_DIM:]
    pairs = len(chunks) * (blocks // 2)
    parts = []
    for start in range(0, acc.shape[1], TILE):
        cut = slice(start, start + TILE)
        s = jnp.dot(ka[: pairs * 256, :], qq[:, cut], preferred_element_type=F32)
        probs = jnp.exp2(s)
        total = acc[HEAD_DIM:, cut] + jnp.sum(probs.reshape(pairs * 32, 8, TILE), axis=0)
        probs = probs.astype(BF16)
        out = acc[:HEAD_DIM, cut]
        for u in range(pairs):
            out = out + jnp.dot(
                va[u], probs[u * 256 : (u + 1) * 256], preferred_element_type=F32
            )
        parts.append(jnp.concatenate([out, total], axis=0))
    return jnp.concatenate(parts, axis=1)


def begin_kernel(qkv, qa_ref, acc_ref, ka, va):
    blocks, steps, _, lanes = qkv.shape
    nq = blocks * lanes

    for t in range(steps):
        qa = qa_ref.at[t]
        for b in range(blocks):
            parts = split3(qkv[b, t, :HEAD_DIM, :].astype(F32) * (0.25 * LOG2E))
            qa[:48, b * lanes : (b + 1) * lanes] = jnp.concatenate(parts, axis=0)
        k = jnp.concatenate([qkv[0, t, HEAD_DIM:32, :], qkv[1, t, HEAD_DIM:32, :]], axis=1)
        k = jnp.concatenate([k, k, k], axis=0).T
        sample = jnp.dot(k, qa[:48, :], preferred_element_type=F32)
        shift = split3(-jnp.max(sample, axis=0, keepdims=True))
        row = lax.broadcasted_iota(jnp.int32, (16, nq), 0)
        rows = jnp.zeros((16, nq), F32)
        for i, part in enumerate(shift):
            rows = jnp.where(row == i, part.astype(F32), rows)
        qa[48:, :] = rows.astype(BF16)
        acc_ref[t] = absorb(t, qa[...], jnp.zeros((ROWS, nq), F32), [qkv], ka.at[t], va.at[t])


def more_kernel(qa, acc_in, *refs):
    chunks, acc_out, ka, va = refs[:-3], refs[-3], refs[-2], refs[-1]

    for t in range(qa.shape[0]):
        acc_out[t] = absorb(t, qa[t], acc_in[t], chunks, ka.at[t], va.at[t])


def end_kernel(count, qa, acc_in, qkv, *refs):
    chunks, out_ref, ka, va = refs[:-3], refs[-3], refs[-2], refs[-1]
    late = chunks[len(chunks) - count :]
    blocks, steps, _, lanes = qkv.shape
    nq = blocks * lanes

    def store(t, value):
        for b in range(blocks):
            out_ref[b, t] = value[:, b * lanes : (b + 1) * lanes].astype(BF16)

    bad = jnp.zeros((1, nq), F32)
    for t in range(steps):
        acc = absorb(t, qa[t], acc_in[t], late, ka.at[t], va.at[t])
        total = jnp.sum(acc[HEAD_DIM:], axis=0, keepdims=True)
        store(t, acc[:HEAD_DIM] / total)
        good = (total >= LOWEST) & (total <= HIGHEST)
        bad = jnp.maximum(bad, jnp.where(good, 0.0, 1.0))

    @pl.when(jnp.max(bad) > 0.0)
    def exact():
        def step(t, carry):
            qq = jnp.concatenate([qkv[b, t, :HEAD_DIM, :] for b in range(blocks)], axis=1)

            def scores(chunk, i):
                k = chunk[i, t, -32:-HEAD_DIM].T
                return jnp.dot(k, qq, preferred_element_type=F32) * 0.25

            top = jnp.full((1, nq), -jnp.inf, F32)
            for chunk in (qkv, *chunks):

                def largest(i, top):
                    return jnp.maximum(top, jnp.max(scores(chunk, i), axis=0, keepdims=True))

                top = lax.fori_loop(0, blocks, largest, top)
            sums = (jnp.zeros((HEAD_DIM, nq), F32), jnp.zeros((1, nq), F32))
            for chunk in (qkv, *chunks):

                def block(i, sums):
                    out, total = sums
                    p = jnp.exp(scores(chunk, i) - top)
                    total = total + jnp.sum(p, axis=0, keepdims=True)
                    v = chunk[i, t, -HEAD_DIM:]
                    return out + jnp.dot(v, p.astype(BF16), preferred_element_type=F32), total

                sums = lax.fori_loop(0, blocks, block, sums)
            store(t, sums[0] / sums[1])
            return carry

        lax.fori_loop(0, steps, step, 0)


def attention(kernel, operands, out_shape, chunks, aliases={}):
    shape = operands[-1].shape
    near, steps, _, sens = shape
    keys = chunks * near * sens
    return pl.pallas_call(
        kernel,
        out_shape=out_shape,
        in_specs=[VMEM] * len(operands),
        out_specs=jax.tree.map(lambda _: VMEM, out_shape),
        scratch_shapes=[
            pltpu.VMEM((steps, keys, 64), BF16),
            pltpu.VMEM((steps, keys // 256, HEAD_DIM, 256), BF16),
        ],
        input_output_aliases=aliases,
        cost_estimate=pl.CostEstimate(
            flops=2 * keys * near * sens * steps * 256 * 2,
            bytes_accessed=0,
            transcendentals=keys * near * sens * steps,
        ),
        compiler_params=pltpu.CompilerParams(vmem_limit_bytes=48 << 20),
    )(*operands)


def last_kernel(mirror, attended, hidden, out_w, gain, out_ref):
    flip = mirror[0]
    heads, steps, dim, sens = attended.shape
    width = heads * dim
    for t in range(steps):
        rows = jnp.concatenate([attended[h ^ flip, t] for h in range(heads)], axis=0).T
        mixed = jnp.dot(rows, out_w[...], preferred_element_type=F32)
        mixed = mixed + hidden[t * sens : (t + 1) * sens, :].astype(F32)
        mean = jnp.mean(mixed, axis=-1, keepdims=True)
        centred = mixed - mean
        var = jnp.mean(centred * centred, axis=-1, keepdims=True)
        out_ref[t] = (centred / jnp.sqrt(var + 1e-5) * gain[...]).astype(BF16)


def local(series, conv_weight, qk_weight, value_weight, out_weight, norm_gain):
    steps, sens, width = series.shape
    blocks = lax.axis_size(TM)
    mirror = (lax.axis_index("y1") * 4 + lax.axis_index("x1") * 2).astype(jnp.int32).reshape(1)
    earlier = lax.ppermute(series[steps - 2 :], TM, [(i, i + 1) for i in range(blocks - 1)])
    conv_own, gain = pl.pallas_call(
        early_kernel,
        out_shape=(
            jax.ShapeDtypeStruct((steps * sens, 2 * width), F32),
            jax.ShapeDtypeStruct((1, width), F32),
        ),
        in_specs=[VMEM] * 3,
        out_specs=(VMEM, VMEM),
        cost_estimate=pl.CostEstimate(
            flops=2 * 3 * steps * sens * width * 2 * width, bytes_accessed=0, transcendentals=0
        ),
        compiler_params=pltpu.CompilerParams(vmem_limit_bytes=32 << 20),
    )(series, conv_weight, norm_gain.reshape(1, width))
    hidden, qkv = pl.pallas_call(
        first_kernel,
        out_shape=(
            jax.ShapeDtypeStruct((steps * sens, width), BF16),
            jax.ShapeDtypeStruct((HEADS, steps, 3 * HEAD_DIM, sens), BF16),
        ),
        in_specs=[SMEM] + [VMEM] * 6,
        out_specs=(VMEM, VMEM),
        compiler_params=pltpu.CompilerParams(vmem_limit_bytes=32 << 20),
    )(mirror, earlier, series, conv_own, conv_weight, qk_weight, value_weight)
    qkv = lax.all_to_all(qkv, NEAR, 0, 0, tiled=True)
    kv = qkv[:, :, HEAD_DIM:, :]

    def swap(block, mask):
        return lax.ppermute(block, SENSOR, [(i, i ^ mask) for i in range(64)])

    along_z, along_y, along_x = 0b000010, 0b110000, 0b001100
    from_z = swap(kv, along_z)
    from_y = swap(kv, along_y)
    from_x = swap(kv, along_x)
    from_yx = swap(from_y, along_x)
    from_zy = swap(from_z, along_y)
    from_zx = swap(from_z, along_x)
    from_zyx = swap(from_zy, along_x)
    near = qkv.shape[0]
    nq = near * sens
    state = (
        jax.ShapeDtypeStruct((steps, 64, nq), BF16),
        jax.ShapeDtypeStruct((steps, ROWS, nq), F32),
    )
    qa, acc = attention(begin_kernel, (qkv,), state, 1)
    for blocks in ((from_y,), (from_z, from_x), (from_yx, from_zy)):
        acc = attention(more_kernel, (qa, acc, *blocks), state[1], len(blocks), {1: 0})
    attended = attention(
        functools.partial(end_kernel, 2),
        (qa, acc, qkv, from_y, from_z, from_x, from_yx, from_zy, from_zx, from_zyx),
        jax.ShapeDtypeStruct((near, steps, HEAD_DIM, sens), BF16),
        2,
    )
    attended = lax.all_to_all(attended, NEAR, 0, 0, tiled=True)
    return pl.pallas_call(
        last_kernel,
        out_shape=jax.ShapeDtypeStruct((steps, sens, width), BF16),
        in_specs=[SMEM] + [VMEM] * 4,
        out_specs=VMEM,
        compiler_params=pltpu.CompilerParams(vmem_limit_bytes=32 << 20),
    )(mirror, attended, hidden, out_weight, gain)


def solution(mesh):
    fine = Mesh(mesh.devices.reshape((2,) * len(AXES)), AXES)
    spec = P(TM, SENSOR, None)
    return jax.shard_map(
        local,
        mesh=fine,
        in_specs=(spec, P(), P(), P(), P(), P()),
        out_specs=spec,
        check_vma=False,
    )
```

```python
import functools

import jax
import jax.numpy as jnp
from jax import lax
from jax.experimental import pallas as pl
from jax.experimental.pallas import tpu as pltpu
from jax.sharding import Mesh, PartitionSpec as P

F32 = jnp.float32
BF16 = jnp.bfloat16
HEADS = 8
HEAD_DIM = 16
LOG2E = 1.4426950408889634
AXES = ("y1", "y0", "x1", "x0", "z1", "z0", "zh", "core")
SENSOR = AXES[:6]
TM = AXES[6:]
NEAR = ("y0", "x0", "z0")
VMEM = pl.BlockSpec(memory_space=pltpu.VMEM)
SMEM = pl.BlockSpec(memory_space=pltpu.SMEM)
TILE = 512
ROWS = HEAD_DIM + 8
LOWEST = 2.0**-20
HIGHEST = 2.0**100


def split3(x):
    high = x.astype(BF16)
    rest = x - high.astype(F32)
    mid = rest.astype(BF16)
    low = (rest - mid.astype(F32)).astype(BF16)
    return high, mid, low


def early_kernel(series, conv_w, gain, conv_ref, gain_ref):
    steps, sens, width = series.shape
    own = series[...].reshape(steps * sens, width)
    conv_ref[...] = jnp.dot(own, conv_w[0], preferred_element_type=F32)
    for tap in (1, 2):
        rows = (steps - tap) * sens
        conv_ref[tap * sens :, :] += jnp.dot(own[:rows], conv_w[tap], preferred_element_type=F32)
    gain_ref[...] = gain[...]


def first_kernel(mirror, earlier, series, conv_own, conv_w, qk_w, value_w, hidden_ref, qkv_ref):
    flip = mirror[0]
    steps, sens, width = series.shape
    own = series[...].reshape(steps * sens, width)
    before = earlier[...].reshape(2 * sens, width)
    late = jnp.dot(before, conv_w[2], preferred_element_type=F32)
    near = jnp.dot(before[sens:], conv_w[1], preferred_element_type=F32)
    late = late + jnp.concatenate([near, jnp.zeros_like(near)], axis=0)
    conv = conv_own[...]
    conv = jnp.concatenate([conv[: 2 * sens] + late, conv[2 * sens :]], axis=0)
    gate = jax.nn.sigmoid(conv[:, width:])
    hidden = (own.astype(F32) + conv[:, :width] * gate).astype(BF16)
    hidden_ref[...] = hidden
    for part, weight in enumerate((qk_w[0], qk_w[1], value_w[...])):
        rows = jnp.dot(hidden, weight, preferred_element_type=F32).astype(BF16)
        for t in range(steps):
            cols = rows[t * sens : (t + 1) * sens].T
            for h in range(HEADS):
                qkv_ref[h ^ flip, t, part * HEAD_DIM : (part + 1) * HEAD_DIM, :] = cols[
                    h * HEAD_DIM : (h + 1) * HEAD_DIM
                ]


def absorb(t, qq, acc, chunks, ka, va):
    blocks, lanes = chunks[0].shape[0], chunks[0].shape[3]
    one = jnp.ones((16, 2 * lanes), BF16)
    for c, chunk in enumerate(chunks):
        for p in range(blocks // 2):
            kv = jnp.concatenate([chunk[2 * p, t, -32:], chunk[2 * p + 1, t, -32:]], axis=1)
            k = kv[:HEAD_DIM]
            pair = c * (blocks // 2) + p
            ka[pair * 256 : (pair + 1) * 256, :] = jnp.concatenate([k, k, k, one], axis=0).T
            va[pair] = kv[HEAD_DIM:]
    pairs = len(chunks) * (blocks // 2)
    parts = []
    for start in range(0, acc.shape[1], TILE):
        cut = slice(start, start + TILE)
        s = jnp.dot(ka[: pairs * 256, :], qq[:, cut], preferred_element_type=F32)
        probs = jnp.exp2(s)
        total = acc[HEAD_DIM:, cut] + jnp.sum(probs.reshape(pairs * 32, 8, TILE), axis=0)
        probs = probs.astype(BF16)
        out = acc[:HEAD_DIM, cut]
        for u in range(pairs):
            out = out + jnp.dot(
                va[u], probs[u * 256 : (u + 1) * 256], preferred_element_type=F32
            )
        parts.append(jnp.concatenate([out, total], axis=0))
    return jnp.concatenate(parts, axis=1)


def begin_kernel(qkv, qa_ref, acc_ref, ka, va):
    blocks, steps, _, lanes = qkv.shape
    nq = blocks * lanes

    for t in range(steps):
        qa = qa_ref.at[t]
        for b in range(blocks):
            parts = split3(qkv[b, t, :HEAD_DIM, :].astype(F32) * (0.25 * LOG2E))
            qa[:48, b * lanes : (b + 1) * lanes] = jnp.concatenate(parts, axis=0)
        k = jnp.concatenate([qkv[0, t, HEAD_DIM:32, :], qkv[1, t, HEAD_DIM:32, :]], axis=1)
        k = jnp.concatenate([k, k, k], axis=0).T
        sample = jnp.dot(k, qa[:48, :], preferred_element_type=F32)
        shift = split3(-jnp.max(sample, axis=0, keepdims=True))
        row = lax.broadcasted_iota(jnp.int32, (16, nq), 0)
        rows = jnp.zeros((16, nq), F32)
        for i, part in enumerate(shift):
            rows = jnp.where(row == i, part.astype(F32), rows)
        qa[48:, :] = rows.astype(BF16)
        acc_ref[t] = absorb(t, qa[...], jnp.zeros((ROWS, nq), F32), [qkv], ka.at[t], va.at[t])


def more_kernel(qa, acc_in, *refs):
    chunks, acc_out, ka, va = refs[:-3], refs[-3], refs[-2], refs[-1]

    for t in range(qa.shape[0]):
        acc_out[t] = absorb(t, qa[t], acc_in[t], chunks, ka.at[t], va.at[t])


def end_kernel(count, qa, acc_in, qkv, *refs):
    chunks, out_ref, ka, va = refs[:-3], refs[-3], refs[-2], refs[-1]
    late = chunks[len(chunks) - count :]
    blocks, steps, _, lanes = qkv.shape
    nq = blocks * lanes

    def store(t, value):
        for b in range(blocks):
            out_ref[b, t] = value[:, b * lanes : (b + 1) * lanes].astype(BF16)

    bad = jnp.zeros((1, nq), F32)
    for t in range(steps):
        acc = absorb(t, qa[t], acc_in[t], late, ka.at[t], va.at[t])
        total = jnp.sum(acc[HEAD_DIM:], axis=0, keepdims=True)
        store(t, acc[:HEAD_DIM] / total)
        good = (total >= LOWEST) & (total <= HIGHEST)
        bad = jnp.maximum(bad, jnp.where(good, 0.0, 1.0))

    @pl.when(jnp.max(bad) > 0.0)
    def exact():
        def step(t, carry):
            qq = jnp.concatenate([qkv[b, t, :HEAD_DIM, :] for b in range(blocks)], axis=1)

            def scores(chunk, i):
                k = chunk[i, t, -32:-HEAD_DIM].T
                return jnp.dot(k, qq, preferred_element_type=F32) * 0.25

            top = jnp.full((1, nq), -jnp.inf, F32)
            for chunk in (qkv, *chunks):

                def largest(i, top):
                    return jnp.maximum(top, jnp.max(scores(chunk, i), axis=0, keepdims=True))

                top = lax.fori_loop(0, blocks, largest, top)
            sums = (jnp.zeros((HEAD_DIM, nq), F32), jnp.zeros((1, nq), F32))
            for chunk in (qkv, *chunks):

                def block(i, sums):
                    out, total = sums
                    p = jnp.exp(scores(chunk, i) - top)
                    total = total + jnp.sum(p, axis=0, keepdims=True)
                    v = chunk[i, t, -HEAD_DIM:]
                    return out + jnp.dot(v, p.astype(BF16), preferred_element_type=F32), total

                sums = lax.fori_loop(0, blocks, block, sums)
            store(t, sums[0] / sums[1])
            return carry

        lax.fori_loop(0, steps, step, 0)


def attention(kernel, operands, out_shape, chunks, aliases={}):
    shape = operands[-1].shape
    near, steps, _, sens = shape
    keys = chunks * near * sens
    return pl.pallas_call(
        kernel,
        out_shape=out_shape,
        in_specs=[VMEM] * len(operands),
        out_specs=jax.tree.map(lambda _: VMEM, out_shape),
        scratch_shapes=[
            pltpu.VMEM((steps, keys, 64), BF16),
            pltpu.VMEM((steps, keys // 256, HEAD_DIM, 256), BF16),
        ],
        input_output_aliases=aliases,
        cost_estimate=pl.CostEstimate(
            flops=2 * keys * near * sens * steps * 256 * 2,
            bytes_accessed=0,
            transcendentals=keys * near * sens * steps,
        ),
        compiler_params=pltpu.CompilerParams(vmem_limit_bytes=48 << 20),
    )(*operands)


def last_kernel(mirror, attended, hidden, out_w, gain, out_ref):
    flip = mirror[0]
    heads, steps, dim, sens = attended.shape
    width = heads * dim
    for t in range(steps):
        rows = jnp.concatenate([attended[h ^ flip, t] for h in range(heads)], axis=0).T
        mixed = jnp.dot(rows, out_w[...], preferred_element_type=F32)
        mixed = mixed + hidden[t * sens : (t + 1) * sens, :].astype(F32)
        mean = jnp.mean(mixed, axis=-1, keepdims=True)
        centred = mixed - mean
        var = jnp.mean(centred * centred, axis=-1, keepdims=True)
        out_ref[t] = (centred / jnp.sqrt(var + 1e-5) * gain[...]).astype(BF16)


def local(series, conv_weight, qk_weight, value_weight, out_weight, norm_gain):
    steps, sens, width = series.shape
    blocks = lax.axis_size(TM)
    mirror = (lax.axis_index("y1") * 4 + lax.axis_index("x1") * 2).astype(jnp.int32).reshape(1)
    earlier = lax.ppermute(series[steps - 2 :], TM, [(i, i + 1) for i in range(blocks - 1)])
    conv_own, gain = pl.pallas_call(
        early_kernel,
        out_shape=(
            jax.ShapeDtypeStruct((steps * sens, 2 * width), F32),
            jax.ShapeDtypeStruct((1, width), F32),
        ),
        in_specs=[VMEM] * 3,
        out_specs=(VMEM, VMEM),
        cost_estimate=pl.CostEstimate(
            flops=2 * 3 * steps * sens * width * 2 * width, bytes_accessed=0, transcendentals=0
        ),
        compiler_params=pltpu.CompilerParams(vmem_limit_bytes=32 << 20),
    )(series, conv_weight, norm_gain.reshape(1, width))
    hidden, qkv = pl.pallas_call(
        first_kernel,
        out_shape=(
            jax.ShapeDtypeStruct((steps * sens, width), BF16),
            jax.ShapeDtypeStruct((HEADS, steps, 3 * HEAD_DIM, sens), BF16),
        ),
        in_specs=[SMEM] + [VMEM] * 6,
        out_specs=(VMEM, VMEM),
        compiler_params=pltpu.CompilerParams(vmem_limit_bytes=32 << 20),
    )(mirror, earlier, series, conv_own, conv_weight, qk_weight, value_weight)
    qkv = lax.all_to_all(qkv, NEAR, 0, 0, tiled=True)
    kv = qkv[:, :, HEAD_DIM:, :]

    def swap(block, mask):
        return lax.ppermute(block, SENSOR, [(i, i ^ mask) for i in range(64)])

    along_z, along_y, along_x = 0b000010, 0b110000, 0b001100
    from_z = swap(kv, along_z)
    from_y = swap(kv, along_y)
    from_x = swap(kv, along_x)
    from_zy = swap(from_z, along_y)
    from_zx = swap(from_z, along_x)
    from_xy = swap(from_x, along_y)
    from_zyx = swap(from_zy, along_x)
    near = qkv.shape[0]
    nq = near * sens
    state = (
        jax.ShapeDtypeStruct((steps, 64, nq), BF16),
        jax.ShapeDtypeStruct((steps, ROWS, nq), F32),
    )
    qa, acc = attention(begin_kernel, (qkv,), state, 1)
    for blocks in ((from_z, from_y), (from_x, from_xy)):
        acc = attention(more_kernel, (qa, acc, *blocks), state[1], len(blocks), {1: 0})
    attended = attention(
        functools.partial(end_kernel, 3),
        (qa, acc, qkv, from_z, from_y, from_x, from_xy, from_zy, from_zx, from_zyx),
        jax.ShapeDtypeStruct((near, steps, HEAD_DIM, sens), BF16),
        3,
    )
    attended = lax.all_to_all(attended, NEAR, 0, 0, tiled=True)
    return pl.pallas_call(
        last_kernel,
        out_shape=jax.ShapeDtypeStruct((steps, sens, width), BF16),
        in_specs=[SMEM] + [VMEM] * 4,
        out_specs=VMEM,
        compiler_params=pltpu.CompilerParams(vmem_limit_bytes=32 << 20),
    )(mirror, attended, hidden, out_weight, gain)


def solution(mesh):
    fine = Mesh(mesh.devices.reshape((2,) * len(AXES)), AXES)
    spec = P(TM, SENSOR, None)
    return jax.shard_map(
        local,
        mesh=fine,
        in_specs=(spec, P(), P(), P(), P(), P()),
        out_specs=spec,
        check_vma=False,
    )
```

```python
import functools

import jax
import jax.numpy as jnp
from jax import lax
from jax.experimental import pallas as pl
from jax.experimental.pallas import tpu as pltpu
from jax.sharding import Mesh, PartitionSpec as P

F32 = jnp.float32
BF16 = jnp.bfloat16
HEADS = 8
HEAD_DIM = 16
LOG2E = 1.4426950408889634
AXES = ("y1", "y0", "x1", "x0", "z1", "z0", "zh", "core")
SENSOR = AXES[:6]
TM = AXES[6:]
NEAR = ("z0", "y0", "x0")
VMEM = pl.BlockSpec(memory_space=pltpu.VMEM)
SMEM = pl.BlockSpec(memory_space=pltpu.SMEM)
TILE = 512
ROWS = HEAD_DIM + 8
LOWEST = 2.0**-20
HIGHEST = 2.0**100


def split3(x):
    high = x.astype(BF16)
    rest = x - high.astype(F32)
    mid = rest.astype(BF16)
    low = (rest - mid.astype(F32)).astype(BF16)
    return high, mid, low


def early_kernel(series, conv_w, gain, conv_ref, gain_ref):
    steps, sens, width = series.shape
    own = series[...].reshape(steps * sens, width)
    conv_ref[...] = jnp.dot(own, conv_w[0], preferred_element_type=F32)
    for tap in (1, 2):
        rows = (steps - tap) * sens
        conv_ref[tap * sens :, :] += jnp.dot(own[:rows], conv_w[tap], preferred_element_type=F32)
    gain_ref[...] = gain[...]


def first_kernel(mirror, earlier, series, conv_own, conv_w, qk_w, value_w, hidden_ref, qkv_ref):
    flip = mirror[0]
    steps, sens, width = series.shape
    own = series[...].reshape(steps * sens, width)
    before = earlier[...].reshape(2 * sens, width)
    late = jnp.dot(before, conv_w[2], preferred_element_type=F32)
    near = jnp.dot(before[sens:], conv_w[1], preferred_element_type=F32)
    late = late + jnp.concatenate([near, jnp.zeros_like(near)], axis=0)
    conv = conv_own[...]
    conv = jnp.concatenate([conv[: 2 * sens] + late, conv[2 * sens :]], axis=0)
    gate = jax.nn.sigmoid(conv[:, width:])
    hidden = (own.astype(F32) + conv[:, :width] * gate).astype(BF16)
    hidden_ref[...] = hidden
    for part, weight in enumerate((qk_w[0], qk_w[1], value_w[...])):
        rows = jnp.dot(hidden, weight, preferred_element_type=F32).astype(BF16)
        for t in range(steps):
            cols = rows[t * sens : (t + 1) * sens].T
            for h in range(HEADS):
                qkv_ref[h ^ flip, t, part * HEAD_DIM : (part + 1) * HEAD_DIM, :] = cols[
                    h * HEAD_DIM : (h + 1) * HEAD_DIM
                ]


def absorb(t, qq, acc, chunks, ka, va):
    lanes = chunks[0].shape[3]
    one = jnp.ones((16, 2 * lanes), BF16)
    pairs = 0
    for chunk in chunks:
        for p in range(chunk.shape[0] // 2):
            kv = jnp.concatenate([chunk[2 * p, t, -32:], chunk[2 * p + 1, t, -32:]], axis=1)
            k = kv[:HEAD_DIM]
            ka[pairs * 256 : (pairs + 1) * 256, :] = jnp.concatenate([k, k, k, one], axis=0).T
            va[pairs] = kv[HEAD_DIM:]
            pairs += 1
    parts = []
    for start in range(0, acc.shape[1], TILE):
        cut = slice(start, start + TILE)
        s = jnp.dot(ka[: pairs * 256, :], qq[:, cut], preferred_element_type=F32)
        probs = jnp.exp2(s)
        total = acc[HEAD_DIM:, cut] + jnp.sum(probs.reshape(pairs * 32, 8, TILE), axis=0)
        probs = probs.astype(BF16)
        out = acc[:HEAD_DIM, cut]
        for u in range(pairs):
            out = out + jnp.dot(
                va[u], probs[u * 256 : (u + 1) * 256], preferred_element_type=F32
            )
        parts.append(jnp.concatenate([out, total], axis=0))
    return jnp.concatenate(parts, axis=1)


def begin_kernel(qkv, qa_ref, acc_ref, ka, va):
    blocks, steps, _, lanes = qkv.shape
    nq = blocks * lanes

    for t in range(steps):
        qa = qa_ref.at[t]
        for b in range(blocks):
            parts = split3(qkv[b, t, :HEAD_DIM, :].astype(F32) * (0.25 * LOG2E))
            qa[:48, b * lanes : (b + 1) * lanes] = jnp.concatenate(parts, axis=0)
        k = jnp.concatenate([qkv[0, t, HEAD_DIM:32, :], qkv[1, t, HEAD_DIM:32, :]], axis=1)
        k = jnp.concatenate([k, k, k], axis=0).T
        sample = jnp.dot(k, qa[:48, :], preferred_element_type=F32)
        shift = split3(-jnp.max(sample, axis=0, keepdims=True))
        row = lax.broadcasted_iota(jnp.int32, (16, nq), 0)
        rows = jnp.zeros((16, nq), F32)
        for i, part in enumerate(shift):
            rows = jnp.where(row == i, part.astype(F32), rows)
        qa[48:, :] = rows.astype(BF16)
        acc_ref[t] = absorb(t, qa[...], jnp.zeros((ROWS, nq), F32), [qkv], ka.at[t], va.at[t])


def more_kernel(qa, acc_in, *refs):
    chunks, acc_out, ka, va = refs[:-3], refs[-3], refs[-2], refs[-1]

    for t in range(qa.shape[0]):
        acc_out[t] = absorb(t, qa[t], acc_in[t], chunks, ka.at[t], va.at[t])


def end_kernel(count, qa, acc_in, qkv, *refs):
    chunks, out_ref, ka, va = refs[:-3], refs[-3], refs[-2], refs[-1]
    late = chunks[len(chunks) - count :]
    blocks, steps, _, lanes = qkv.shape
    nq = blocks * lanes

    def store(t, value):
        for b in range(blocks):
            out_ref[b, t] = value[:, b * lanes : (b + 1) * lanes].astype(BF16)

    bad = jnp.zeros((1, nq), F32)
    for t in range(steps):
        acc = absorb(t, qa[t], acc_in[t], late, ka.at[t], va.at[t])
        total = jnp.sum(acc[HEAD_DIM:], axis=0, keepdims=True)
        store(t, acc[:HEAD_DIM] / total)
        good = (total >= LOWEST) & (total <= HIGHEST)
        bad = jnp.maximum(bad, jnp.where(good, 0.0, 1.0))

    @pl.when(jnp.max(bad) > 0.0)
    def exact():
        def step(t, carry):
            qq = jnp.concatenate([qkv[b, t, :HEAD_DIM, :] for b in range(blocks)], axis=1)

            def scores(chunk, i):
                k = chunk[i, t, -32:-HEAD_DIM].T
                return jnp.dot(k, qq, preferred_element_type=F32) * 0.25

            top = jnp.full((1, nq), -jnp.inf, F32)
            for chunk in (qkv, *chunks):

                def largest(i, top):
                    return jnp.maximum(top, jnp.max(scores(chunk, i), axis=0, keepdims=True))

                top = lax.fori_loop(0, chunk.shape[0], largest, top)
            sums = (jnp.zeros((HEAD_DIM, nq), F32), jnp.zeros((1, nq), F32))
            for chunk in (qkv, *chunks):

                def block(i, sums):
                    out, total = sums
                    p = jnp.exp(scores(chunk, i) - top)
                    total = total + jnp.sum(p, axis=0, keepdims=True)
                    v = chunk[i, t, -HEAD_DIM:]
                    return out + jnp.dot(v, p.astype(BF16), preferred_element_type=F32), total

                sums = lax.fori_loop(0, chunk.shape[0], block, sums)
            store(t, sums[0] / sums[1])
            return carry

        lax.fori_loop(0, steps, step, 0)


def attention(kernel, operands, out_shape, chunks, shape, aliases={}):
    near, steps, _, sens = shape
    keys = chunks * near * sens
    return pl.pallas_call(
        kernel,
        out_shape=out_shape,
        in_specs=[VMEM] * len(operands),
        out_specs=jax.tree.map(lambda _: VMEM, out_shape),
        scratch_shapes=[
            pltpu.VMEM((steps, keys, 64), BF16),
            pltpu.VMEM((steps, keys // 256, HEAD_DIM, 256), BF16),
        ],
        input_output_aliases=aliases,
        cost_estimate=pl.CostEstimate(
            flops=2 * keys * near * sens * steps * 256 * 2,
            bytes_accessed=0,
            transcendentals=keys * near * sens * steps,
        ),
        compiler_params=pltpu.CompilerParams(vmem_limit_bytes=48 << 20),
    )(*operands)


def last_kernel(mirror, attended, hidden, out_w, gain, out_ref):
    flip = mirror[0]
    heads, steps, dim, sens = attended.shape
    width = heads * dim
    for t in range(steps):
        rows = jnp.concatenate([attended[h ^ flip, t] for h in range(heads)], axis=0).T
        mixed = jnp.dot(rows, out_w[...], preferred_element_type=F32)
        mixed = mixed + hidden[t * sens : (t + 1) * sens, :].astype(F32)
        mean = jnp.mean(mixed, axis=-1, keepdims=True)
        centred = mixed - mean
        var = jnp.mean(centred * centred, axis=-1, keepdims=True)
        out_ref[t] = (centred / jnp.sqrt(var + 1e-5) * gain[...]).astype(BF16)


def local(series, conv_weight, qk_weight, value_weight, out_weight, norm_gain):
    steps, sens, width = series.shape
    blocks = lax.axis_size(TM)
    mirror = (lax.axis_index("y1") * 2 + lax.axis_index("x1") * 1).astype(jnp.int32).reshape(1)
    earlier = lax.ppermute(series[steps - 2 :], TM, [(i, i + 1) for i in range(blocks - 1)])
    conv_own, gain = pl.pallas_call(
        early_kernel,
        out_shape=(
            jax.ShapeDtypeStruct((steps * sens, 2 * width), F32),
            jax.ShapeDtypeStruct((1, width), F32),
        ),
        in_specs=[VMEM] * 3,
        out_specs=(VMEM, VMEM),
        cost_estimate=pl.CostEstimate(
            flops=2 * 3 * steps * sens * width * 2 * width, bytes_accessed=0, transcendentals=0
        ),
        compiler_params=pltpu.CompilerParams(vmem_limit_bytes=32 << 20),
    )(series, conv_weight, norm_gain.reshape(1, width))
    hidden, qkv = pl.pallas_call(
        first_kernel,
        out_shape=(
            jax.ShapeDtypeStruct((steps * sens, width), BF16),
            jax.ShapeDtypeStruct((HEADS, steps, 3 * HEAD_DIM, sens), BF16),
        ),
        in_specs=[SMEM] + [VMEM] * 6,
        out_specs=(VMEM, VMEM),
        compiler_params=pltpu.CompilerParams(vmem_limit_bytes=32 << 20),
    )(mirror, earlier, series, conv_own, conv_weight, qk_weight, value_weight)
    qkv = lax.all_to_all(qkv, NEAR, 0, 0, tiled=True)
    kv = qkv[:, :, HEAD_DIM:, :]

    def swap(block, mask):
        return lax.ppermute(block, SENSOR, [(i, i ^ mask) for i in range(64)])

    along_z, along_y, along_x = 0b000010, 0b110000, 0b001100
    from_z = swap(kv, along_z)
    from_y = swap(kv, along_y)
    from_x = swap(kv, along_x)
    from_zy = swap(from_z, along_y)
    beyond_x = swap(jnp.concatenate([from_z, from_y], axis=0), along_x)
    from_zyx = swap(from_zy, along_x)
    near = qkv.shape[0]
    nq = near * sens
    state = (
        jax.ShapeDtypeStruct((steps, 64, nq), BF16),
        jax.ShapeDtypeStruct((steps, ROWS, nq), F32),
    )
    shape = kv.shape
    qa, acc = attention(begin_kernel, (qkv,), state, 1, shape)
    for pair in ((from_z, from_y), (from_x, from_zy)):
        acc = attention(more_kernel, (qa, acc, *pair), state[1], 2, shape, {1: 0})
    attended = attention(
        functools.partial(end_kernel, 2),
        (qa, acc, qkv, from_z, from_y, from_x, from_zy, beyond_x, from_zyx),
        jax.ShapeDtypeStruct((near, steps, HEAD_DIM, sens), BF16),
        3,
        shape,
    )
    attended = lax.all_to_all(attended, NEAR, 0, 0, tiled=True)
    return pl.pallas_call(
        last_kernel,
        out_shape=jax.ShapeDtypeStruct((steps, sens, width), BF16),
        in_specs=[SMEM] + [VMEM] * 4,
        out_specs=VMEM,
        compiler_params=pltpu.CompilerParams(vmem_limit_bytes=32 << 20),
    )(mirror, attended, hidden, out_weight, gain)


def solution(mesh):
    fine = Mesh(mesh.devices.reshape((2,) * len(AXES)), AXES)
    spec = P(TM, SENSOR, None)
    return jax.shard_map(
        local,
        mesh=fine,
        in_specs=(spec, P(), P(), P(), P(), P()),
        out_specs=spec,
        check_vma=False,
    )
```

```python
import functools

import jax
import jax.numpy as jnp
from jax import lax
from jax.experimental import pallas as pl
from jax.experimental.pallas import tpu as pltpu
from jax.sharding import Mesh, PartitionSpec as P

F32 = jnp.float32
BF16 = jnp.bfloat16
HEADS = 8
HEAD_DIM = 16
LOG2E = 1.4426950408889634
AXES = ("y1", "y0", "x1", "x0", "z1", "z0", "zh", "core")
SENSOR = AXES[:6]
TM = AXES[6:]
NEAR = ("z0", "y0", "x0")
VMEM = pl.BlockSpec(memory_space=pltpu.VMEM)
SMEM = pl.BlockSpec(memory_space=pltpu.SMEM)
TILE = 512
ROWS = HEAD_DIM + 8
LOWEST = 2.0**-20
HIGHEST = 2.0**100


def split3(x):
    high = x.astype(BF16)
    rest = x - high.astype(F32)
    mid = rest.astype(BF16)
    low = (rest - mid.astype(F32)).astype(BF16)
    return high, mid, low


def project(conv, own, qk_w, value_w, flip, steps, hidden_ref, qkv_ref):
    sens = qkv_ref.shape[-1]
    width = own.shape[1]
    gate = jax.nn.sigmoid(conv[:, width:])
    hidden = (own.astype(F32) + conv[:, :width] * gate).astype(BF16)
    hidden_ref[steps[0] * sens : (steps[-1] + 1) * sens, :] = hidden
    for part, weight in enumerate((qk_w[0], qk_w[1], value_w[...])):
        rows = jnp.dot(hidden, weight, preferred_element_type=F32).astype(BF16)
        for i, t in enumerate(steps):
            cols = rows[i * sens : (i + 1) * sens].T
            for h in range(HEADS):
                qkv_ref[h ^ flip, t, part * HEAD_DIM : (part + 1) * HEAD_DIM, :] = cols[
                    h * HEAD_DIM : (h + 1) * HEAD_DIM
                ]


def early_kernel(
    mirror, series, conv_w, qk_w, value_w, gain, conv_ref, gain_ref, hidden_ref, qkv_ref
):
    steps, sens, width = series.shape
    own = series[...].reshape(steps * sens, width)
    conv = jnp.dot(own, conv_w[0], preferred_element_type=F32)
    for tap in (1, 2):
        rows = (steps - tap) * sens
        late = jnp.dot(own[:rows], conv_w[tap], preferred_element_type=F32)
        conv = jnp.concatenate([conv[: tap * sens], conv[tap * sens :] + late], axis=0)
    gain_ref[...] = gain[...]
    conv_ref[...] = conv[: 2 * sens]
    free = list(range(2, steps))
    project(
        conv[2 * sens :], own[2 * sens :], qk_w, value_w, mirror[0], free, hidden_ref, qkv_ref
    )


def first_kernel(
    mirror, earlier, series, conv_own, conv_w, qk_w, value_w, hidden_in, qkv_in, hidden_ref, qkv_ref
):
    steps, sens, width = series.shape
    own = series[:2].reshape(2 * sens, width)
    before = earlier[...].reshape(2 * sens, width)
    late = jnp.dot(before, conv_w[2], preferred_element_type=F32)
    near = jnp.dot(before[sens:], conv_w[1], preferred_element_type=F32)
    late = late + jnp.concatenate([near, jnp.zeros_like(near)], axis=0)
    project(conv_own[...] + late, own, qk_w, value_w, mirror[0], [0, 1], hidden_ref, qkv_ref)


def absorb(t, qq, acc, chunks, ka, va):
    lanes = chunks[0].shape[3]
    one = jnp.ones((16, 2 * lanes), BF16)
    pairs = 0
    for chunk in chunks:
        for p in range(chunk.shape[0] // 2):
            kv = jnp.concatenate([chunk[2 * p, t, -32:], chunk[2 * p + 1, t, -32:]], axis=1)
            k = kv[:HEAD_DIM]
            ka[pairs * 256 : (pairs + 1) * 256, :] = jnp.concatenate([k, k, k, one], axis=0).T
            va[pairs] = kv[HEAD_DIM:]
            pairs += 1
    parts = []
    for start in range(0, acc.shape[1], TILE):
        cut = slice(start, start + TILE)
        s = jnp.dot(ka[: pairs * 256, :], qq[:, cut], preferred_element_type=F32)
        probs = jnp.exp2(s)
        total = acc[HEAD_DIM:, cut] + jnp.sum(probs.reshape(pairs * 32, 8, TILE), axis=0)
        probs = probs.astype(BF16)
        out = acc[:HEAD_DIM, cut]
        for u in range(pairs):
            out = out + jnp.dot(
                va[u], probs[u * 256 : (u + 1) * 256], preferred_element_type=F32
            )
        parts.append(jnp.concatenate([out, total], axis=0))
    return jnp.concatenate(parts, axis=1)


def begin_kernel(qkv, qa_ref, acc_ref, ka, va):
    blocks, steps, _, lanes = qkv.shape
    nq = blocks * lanes

    for t in range(steps):
        qa = qa_ref.at[t]
        for b in range(blocks):
            parts = split3(qkv[b, t, :HEAD_DIM, :].astype(F32) * (0.25 * LOG2E))
            qa[:48, b * lanes : (b + 1) * lanes] = jnp.concatenate(parts, axis=0)
        k = qkv[0, t, HEAD_DIM:32, :]
        k = jnp.concatenate([k, k, k], axis=0).T
        sample = jnp.dot(k, qa[:48, :], preferred_element_type=F32)
        shift = split3(-jnp.max(sample, axis=0, keepdims=True))
        row = lax.broadcasted_iota(jnp.int32, (16, nq), 0)
        rows = jnp.zeros((16, nq), F32)
        for i, part in enumerate(shift):
            rows = jnp.where(row == i, part.astype(F32), rows)
        qa[48:, :] = rows.astype(BF16)
        acc_ref[t] = absorb(t, qa[...], jnp.zeros((ROWS, nq), F32), [qkv], ka.at[t], va.at[t])


def more_kernel(qa, acc_in, *refs):
    chunks, acc_out, ka, va = refs[:-3], refs[-3], refs[-2], refs[-1]

    for t in range(qa.shape[0]):
        acc_out[t] = absorb(t, qa[t], acc_in[t], chunks, ka.at[t], va.at[t])


def end_kernel(count, qa, acc_in, qkv, *refs):
    chunks, out_ref, ka, va = refs[:-3], refs[-3], refs[-2], refs[-1]
    late = chunks[len(chunks) - count :]
    blocks, steps, _, lanes = qkv.shape
    nq = blocks * lanes

    def store(t, value):
        for b in range(blocks):
            out_ref[b, t] = value[:, b * lanes : (b + 1) * lanes].astype(BF16)

    bad = jnp.zeros((1, nq), F32)
    for t in range(steps):
        acc = absorb(t, qa[t], acc_in[t], late, ka.at[t], va.at[t])
        total = jnp.sum(acc[HEAD_DIM:], axis=0, keepdims=True)
        store(t, acc[:HEAD_DIM] / total)
        good = (total >= LOWEST) & (total <= HIGHEST)
        bad = jnp.maximum(bad, jnp.where(good, 0.0, 1.0))

    @pl.when(jnp.max(bad) > 0.0)
    def exact():
        def step(t, carry):
            qq = jnp.concatenate([qkv[b, t, :HEAD_DIM, :] for b in range(blocks)], axis=1)

            def scores(chunk, i):
                k = chunk[i, t, -32:-HEAD_DIM].T
                return jnp.dot(k, qq, preferred_element_type=F32) * 0.25

            top = jnp.full((1, nq), -jnp.inf, F32)
            for chunk in (qkv, *chunks):

                def largest(i, top):
                    return jnp.maximum(top, jnp.max(scores(chunk, i), axis=0, keepdims=True))

                top = lax.fori_loop(0, chunk.shape[0], largest, top)
            sums = (jnp.zeros((HEAD_DIM, nq), F32), jnp.zeros((1, nq), F32))
            for chunk in (qkv, *chunks):

                def block(i, sums):
                    out, total = sums
                    p = jnp.exp(scores(chunk, i) - top)
                    total = total + jnp.sum(p, axis=0, keepdims=True)
                    v = chunk[i, t, -HEAD_DIM:]
                    return out + jnp.dot(v, p.astype(BF16), preferred_element_type=F32), total

                sums = lax.fori_loop(0, chunk.shape[0], block, sums)
            store(t, sums[0] / sums[1])
            return carry

        lax.fori_loop(0, steps, step, 0)


def attention(kernel, operands, out_shape, chunks, shape, aliases={}):
    near, steps, _, sens = shape
    keys = chunks * near * sens
    return pl.pallas_call(
        kernel,
        out_shape=out_shape,
        in_specs=[VMEM] * len(operands),
        out_specs=jax.tree.map(lambda _: VMEM, out_shape),
        scratch_shapes=[
            pltpu.VMEM((steps, keys, 64), BF16),
            pltpu.VMEM((steps, keys // 256, HEAD_DIM, 256), BF16),
        ],
        input_output_aliases=aliases,
        cost_estimate=pl.CostEstimate(
            flops=2 * keys * near * sens * steps * 256 * 2,
            bytes_accessed=0,
            transcendentals=keys * near * sens * steps,
        ),
        compiler_params=pltpu.CompilerParams(vmem_limit_bytes=48 << 20),
    )(*operands)


def last_kernel(mirror, attended, hidden, out_w, gain, out_ref):
    flip = mirror[0]
    heads, steps, dim, sens = attended.shape
    width = heads * dim
    for t in range(steps):
        rows = jnp.concatenate([attended[h ^ flip, t] for h in range(heads)], axis=0).T
        mixed = jnp.dot(rows, out_w[...], preferred_element_type=F32)
        mixed = mixed + hidden[t * sens : (t + 1) * sens, :].astype(F32)
        mean = jnp.mean(mixed, axis=-1, keepdims=True)
        centred = mixed - mean
        var = jnp.mean(centred * centred, axis=-1, keepdims=True)
        out_ref[t] = (centred / jnp.sqrt(var + 1e-5) * gain[...]).astype(BF16)


def local(series, conv_weight, qk_weight, value_weight, out_weight, norm_gain):
    steps, sens, width = series.shape
    blocks = lax.axis_size(TM)
    mirror = (lax.axis_index("y1") * 2 + lax.axis_index("x1") * 1).astype(jnp.int32).reshape(1)
    earlier = lax.ppermute(series[steps - 2 :], TM, [(i, i + 1) for i in range(blocks - 1)])
    made = (
        jax.ShapeDtypeStruct((steps * sens, width), BF16),
        jax.ShapeDtypeStruct((HEADS, steps, 3 * HEAD_DIM, sens), BF16),
    )
    conv_own, gain, hidden, qkv = pl.pallas_call(
        early_kernel,
        out_shape=(
            jax.ShapeDtypeStruct((2 * sens, 2 * width), F32),
            jax.ShapeDtypeStruct((1, width), F32),
            *made,
        ),
        in_specs=[SMEM] + [VMEM] * 5,
        out_specs=(VMEM,) * 4,
        cost_estimate=pl.CostEstimate(
            flops=2 * 3 * steps * sens * width * 2 * width, bytes_accessed=0, transcendentals=0
        ),
        compiler_params=pltpu.CompilerParams(vmem_limit_bytes=32 << 20),
    )(mirror, series, conv_weight, qk_weight, value_weight, norm_gain.reshape(1, width))
    hidden, qkv = pl.pallas_call(
        first_kernel,
        out_shape=made,
        in_specs=[SMEM] + [VMEM] * 8,
        out_specs=(VMEM, VMEM),
        input_output_aliases={7: 0, 8: 1},
        compiler_params=pltpu.CompilerParams(vmem_limit_bytes=32 << 20),
    )(mirror, earlier, series, conv_own, conv_weight, qk_weight, value_weight, hidden, qkv)
    qkv = lax.all_to_all(qkv, NEAR, 0, 0, tiled=True)
    kv = qkv[:, :, HEAD_DIM:, :]

    def swap(block, mask):
        return lax.ppermute(block, SENSOR, [(i, i ^ mask) for i in range(64)])

    along_z, along_y, along_x = 0b000010, 0b110000, 0b001100
    from_z = swap(kv, along_z)
    from_y = swap(kv, along_y)
    from_x = swap(kv, along_x)
    from_zy = swap(from_z, along_y)
    beyond_x = swap(jnp.concatenate([from_z, from_y], axis=0), along_x)
    from_zyx = swap(from_zy, along_x)
    near = qkv.shape[0]
    nq = near * sens
    state = (
        jax.ShapeDtypeStruct((steps, 64, nq), BF16),
        jax.ShapeDtypeStruct((steps, ROWS, nq), F32),
    )
    shape = kv.shape
    qa, acc = attention(begin_kernel, (qkv,), state, 1, shape)
    for pair in ((from_z, from_y), (from_x, from_zy)):
        acc = attention(more_kernel, (qa, acc, *pair), state[1], 2, shape, {1: 0})
    attended = attention(
        functools.partial(end_kernel, 2),
        (qa, acc, qkv, from_z, from_y, from_x, from_zy, beyond_x, from_zyx),
        jax.ShapeDtypeStruct((near, steps, HEAD_DIM, sens), BF16),
        3,
        shape,
    )
    attended = lax.all_to_all(attended, NEAR, 0, 0, tiled=True)
    return pl.pallas_call(
        last_kernel,
        out_shape=jax.ShapeDtypeStruct((steps, sens, width), BF16),
        in_specs=[SMEM] + [VMEM] * 4,
        out_specs=VMEM,
        compiler_params=pltpu.CompilerParams(vmem_limit_bytes=32 << 20),
    )(mirror, attended, hidden, out_weight, gain)


def solution(mesh):
    fine = Mesh(mesh.devices.reshape((2,) * len(AXES)), AXES)
    spec = P(TM, SENSOR, None)
    return jax.shard_map(
        local,
        mesh=fine,
        in_specs=(spec, P(), P(), P(), P(), P()),
        out_specs=spec,
        check_vma=False,
    )
```

```python
import functools

import jax
import jax.numpy as jnp
from jax import lax
from jax.experimental import pallas as pl
from jax.experimental.pallas import tpu as pltpu
from jax.sharding import Mesh, PartitionSpec as P

F32 = jnp.float32
BF16 = jnp.bfloat16
HEADS = 8
HEAD_DIM = 16
LOG2E = 1.4426950408889634
AXES = ("y1", "y0", "x1", "x0", "z1", "z0", "zh", "core")
SENSOR = AXES[:6]
TM = AXES[6:]
NEAR = ("z0", "y0", "x0")
VMEM = pl.BlockSpec(memory_space=pltpu.VMEM)
SMEM = pl.BlockSpec(memory_space=pltpu.SMEM)
TILE = 512
ROWS = HEAD_DIM + 8
LOWEST = 2.0**-20
HIGHEST = 2.0**100


def split3(x):
    high = x.astype(BF16)
    rest = x - high.astype(F32)
    mid = rest.astype(BF16)
    low = (rest - mid.astype(F32)).astype(BF16)
    return high, mid, low


def project(conv, own, qk_w, value_w, flip, steps, hidden_ref, qkv_ref):
    sens = qkv_ref.shape[-1]
    width = own.shape[1]
    gate = jax.nn.sigmoid(conv[:, width:])
    hidden = (own.astype(F32) + conv[:, :width] * gate).astype(BF16)
    hidden_ref[steps[0] * sens : (steps[-1] + 1) * sens, :] = hidden
    for part, weight in enumerate((qk_w[0], qk_w[1], value_w[...])):
        rows = jnp.dot(hidden, weight, preferred_element_type=F32).astype(BF16)
        for i, t in enumerate(steps):
            cols = rows[i * sens : (i + 1) * sens].T
            for h in range(HEADS):
                qkv_ref[h ^ flip, t, part * HEAD_DIM : (part + 1) * HEAD_DIM, :] = cols[
                    h * HEAD_DIM : (h + 1) * HEAD_DIM
                ]


def early_kernel(
    mirror, series, conv_w, qk_w, value_w, gain, conv_ref, gain_ref, hidden_ref, qkv_ref
):
    steps, sens, width = series.shape
    own = series[...].reshape(steps * sens, width)
    conv = jnp.dot(own, conv_w[0], preferred_element_type=F32)
    for tap in (1, 2):
        rows = (steps - tap) * sens
        late = jnp.dot(own[:rows], conv_w[tap], preferred_element_type=F32)
        conv = jnp.concatenate([conv[: tap * sens], conv[tap * sens :] + late], axis=0)
    gain_ref[...] = gain[...]
    conv_ref[...] = conv[: 2 * sens]
    free = list(range(2, steps))
    project(
        conv[2 * sens :], own[2 * sens :], qk_w, value_w, mirror[0], free, hidden_ref, qkv_ref
    )


def first_kernel(
    mirror, earlier, series, conv_own, conv_w, qk_w, value_w, hidden_in, qkv_in, hidden_ref, qkv_ref
):
    steps, sens, width = series.shape
    own = series[:2].reshape(2 * sens, width)
    before = earlier[...].reshape(2 * sens, width)
    late = jnp.dot(before, conv_w[2], preferred_element_type=F32)
    near = jnp.dot(before[sens:], conv_w[1], preferred_element_type=F32)
    late = late + jnp.concatenate([near, jnp.zeros_like(near)], axis=0)
    project(conv_own[...] + late, own, qk_w, value_w, mirror[0], [0, 1], hidden_ref, qkv_ref)


def absorb(t, qq, acc, chunks, ka, va):
    lanes = chunks[0].shape[3]
    one = jnp.ones((16, 2 * lanes), BF16)
    pairs = 0
    for chunk in chunks:
        for p in range(chunk.shape[0] // 2):
            kv = jnp.concatenate([chunk[2 * p, t, -32:], chunk[2 * p + 1, t, -32:]], axis=1)
            k = kv[:HEAD_DIM]
            ka[pairs * 256 : (pairs + 1) * 256, :] = jnp.concatenate([k, k, k, one], axis=0).T
            va[pairs] = kv[HEAD_DIM:]
            pairs += 1
    parts = []
    for start in range(0, acc.shape[1], TILE):
        cut = slice(start, start + TILE)
        s = jnp.dot(ka[: pairs * 256, :], qq[:, cut], preferred_element_type=F32)
        probs = jnp.exp2(s)
        total = acc[HEAD_DIM:, cut] + jnp.sum(probs.reshape(pairs * 32, 8, TILE), axis=0)
        probs = probs.astype(BF16)
        out = acc[:HEAD_DIM, cut]
        for u in range(pairs):
            out = out + jnp.dot(
                va[u], probs[u * 256 : (u + 1) * 256], preferred_element_type=F32
            )
        parts.append(jnp.concatenate([out, total], axis=0))
    return jnp.concatenate(parts, axis=1)


def begin_kernel(qkv, qa_ref, acc_ref, ka, va):
    blocks, steps, _, lanes = qkv.shape
    nq = blocks * lanes

    for t in range(steps):
        qa = qa_ref.at[t]
        for b in range(blocks):
            parts = split3(qkv[b, t, :HEAD_DIM, :].astype(F32) * (0.25 * LOG2E))
            qa[:48, b * lanes : (b + 1) * lanes] = jnp.concatenate(parts, axis=0)
        k = qkv[0, t, HEAD_DIM:32, :]
        k = jnp.concatenate([k, k, k], axis=0).T
        sample = jnp.dot(k, qa[:48, :], preferred_element_type=F32)
        shift = split3(-jnp.max(sample, axis=0, keepdims=True))
        row = lax.broadcasted_iota(jnp.int32, (16, nq), 0)
        rows = jnp.zeros((16, nq), F32)
        for i, part in enumerate(shift):
            rows = jnp.where(row == i, part.astype(F32), rows)
        qa[48:, :] = rows.astype(BF16)
        acc_ref[t] = absorb(t, qa[...], jnp.zeros((ROWS, nq), F32), [qkv], ka.at[t], va.at[t])


def more_kernel(qa, acc_in, *refs):
    chunks, acc_out, ka, va = refs[:-3], refs[-3], refs[-2], refs[-1]

    for t in range(qa.shape[0]):
        acc_out[t] = absorb(t, qa[t], acc_in[t], chunks, ka.at[t], va.at[t])


def end_kernel(count, qa, acc_in, qkv, *refs):
    chunks, out_ref, ka, va = refs[:-3], refs[-3], refs[-2], refs[-1]
    late = chunks[len(chunks) - count :]
    blocks, steps, _, lanes = qkv.shape
    nq = blocks * lanes

    def store(t, value):
        for b in range(blocks):
            out_ref[b, t] = value[:, b * lanes : (b + 1) * lanes].astype(BF16)

    bad = jnp.zeros((1, nq), F32)
    for t in range(steps):
        acc = absorb(t, qa[t], acc_in[t], late, ka.at[t], va.at[t])
        total = jnp.sum(acc[HEAD_DIM:], axis=0, keepdims=True)
        store(t, acc[:HEAD_DIM] / total)
        good = (total >= LOWEST) & (total <= HIGHEST)
        bad = jnp.maximum(bad, jnp.where(good, 0.0, 1.0))

    @pl.when(jnp.max(bad) > 0.0)
    def exact():
        def step(t, carry):
            qq = jnp.concatenate([qkv[b, t, :HEAD_DIM, :] for b in range(blocks)], axis=1)

            def scores(chunk, i):
                k = chunk[i, t, -32:-HEAD_DIM].T
                return jnp.dot(k, qq, preferred_element_type=F32) * 0.25

            top = jnp.full((1, nq), -jnp.inf, F32)
            for chunk in (qkv, *chunks):

                def largest(i, top):
                    return jnp.maximum(top, jnp.max(scores(chunk, i), axis=0, keepdims=True))

                top = lax.fori_loop(0, chunk.shape[0], largest, top)
            sums = (jnp.zeros((HEAD_DIM, nq), F32), jnp.zeros((1, nq), F32))
            for chunk in (qkv, *chunks):

                def block(i, sums):
                    out, total = sums
                    p = jnp.exp(scores(chunk, i) - top)
                    total = total + jnp.sum(p, axis=0, keepdims=True)
                    v = chunk[i, t, -HEAD_DIM:]
                    return out + jnp.dot(v, p.astype(BF16), preferred_element_type=F32), total

                sums = lax.fori_loop(0, chunk.shape[0], block, sums)
            store(t, sums[0] / sums[1])
            return carry

        lax.fori_loop(0, steps, step, 0)


def attention(kernel, operands, out_shape, chunks, shape, aliases={}):
    near, steps, _, sens = shape
    keys = chunks * near * sens
    return pl.pallas_call(
        kernel,
        out_shape=out_shape,
        in_specs=[VMEM] * len(operands),
        out_specs=jax.tree.map(lambda _: VMEM, out_shape),
        scratch_shapes=[
            pltpu.VMEM((steps, keys, 64), BF16),
            pltpu.VMEM((steps, keys // 256, HEAD_DIM, 256), BF16),
        ],
        input_output_aliases=aliases,
        cost_estimate=pl.CostEstimate(
            flops=2 * keys * near * sens * steps * 256 * 2,
            bytes_accessed=0,
            transcendentals=keys * near * sens * steps,
        ),
        compiler_params=pltpu.CompilerParams(vmem_limit_bytes=48 << 20),
    )(*operands)


def last_kernel(mirror, attended, hidden, out_w, gain, out_ref):
    flip = mirror[0]
    heads, steps, dim, sens = attended.shape
    width = heads * dim
    cols = [
        jnp.concatenate([attended[h ^ flip, t] for h in range(heads)], axis=0)
        for t in range(steps)
    ]
    rows = jnp.concatenate(cols, axis=1).T
    mixed = jnp.dot(rows, out_w[...], preferred_element_type=F32) + hidden[...].astype(F32)
    mean = jnp.mean(mixed, axis=-1, keepdims=True)
    centred = mixed - mean
    var = jnp.mean(centred * centred, axis=-1, keepdims=True)
    normed = (centred / jnp.sqrt(var + 1e-5) * gain[...]).astype(BF16)
    out_ref[...] = normed.reshape(steps, sens, heads * dim)


def local(series, conv_weight, qk_weight, value_weight, out_weight, norm_gain):
    steps, sens, width = series.shape
    blocks = lax.axis_size(TM)
    mirror = (lax.axis_index("y1") * 2 + lax.axis_index("x1") * 1).astype(jnp.int32).reshape(1)
    earlier = lax.ppermute(series[steps - 2 :], TM, [(i, i + 1) for i in range(blocks - 1)])
    made = (
        jax.ShapeDtypeStruct((steps * sens, width), BF16),
        jax.ShapeDtypeStruct((HEADS, steps, 3 * HEAD_DIM, sens), BF16),
    )
    conv_own, gain, hidden, qkv = pl.pallas_call(
        early_kernel,
        out_shape=(
            jax.ShapeDtypeStruct((2 * sens, 2 * width), F32),
            jax.ShapeDtypeStruct((1, width), F32),
            *made,
        ),
        in_specs=[SMEM] + [VMEM] * 5,
        out_specs=(VMEM,) * 4,
        cost_estimate=pl.CostEstimate(
            flops=2 * 3 * steps * sens * width * 2 * width, bytes_accessed=0, transcendentals=0
        ),
        compiler_params=pltpu.CompilerParams(vmem_limit_bytes=32 << 20),
    )(mirror, series, conv_weight, qk_weight, value_weight, norm_gain.reshape(1, width))
    hidden, qkv = pl.pallas_call(
        first_kernel,
        out_shape=made,
        in_specs=[SMEM] + [VMEM] * 8,
        out_specs=(VMEM, VMEM),
        input_output_aliases={7: 0, 8: 1},
        compiler_params=pltpu.CompilerParams(vmem_limit_bytes=32 << 20),
    )(mirror, earlier, series, conv_own, conv_weight, qk_weight, value_weight, hidden, qkv)
    qkv = lax.all_to_all(qkv, NEAR, 0, 0, tiled=True)
    kv = qkv[:, :, HEAD_DIM:, :]

    def swap(block, mask):
        return lax.ppermute(block, SENSOR, [(i, i ^ mask) for i in range(64)])

    along_z, along_y, along_x = 0b000010, 0b110000, 0b001100
    from_z = swap(kv, along_z)
    from_y = swap(kv, along_y)
    from_x = swap(kv, along_x)
    from_zy = swap(from_z, along_y)
    beyond_x = swap(jnp.concatenate([from_z, from_y], axis=0), along_x)
    from_zyx = swap(from_zy, along_x)
    near = qkv.shape[0]
    nq = near * sens
    state = (
        jax.ShapeDtypeStruct((steps, 64, nq), BF16),
        jax.ShapeDtypeStruct((steps, ROWS, nq), F32),
    )
    shape = kv.shape
    qa, acc = attention(begin_kernel, (qkv,), state, 1, shape)
    for pair in ((from_z, from_y), (from_x, from_zy)):
        acc = attention(more_kernel, (qa, acc, *pair), state[1], 2, shape, {1: 0})
    attended = attention(
        functools.partial(end_kernel, 2),
        (qa, acc, qkv, from_z, from_y, from_x, from_zy, beyond_x, from_zyx),
        jax.ShapeDtypeStruct((near, steps, HEAD_DIM, sens), BF16),
        3,
        shape,
    )
    attended = lax.all_to_all(attended, NEAR, 0, 0, tiled=True)
    return pl.pallas_call(
        last_kernel,
        out_shape=jax.ShapeDtypeStruct((steps, sens, width), BF16),
        in_specs=[SMEM] + [VMEM] * 4,
        out_specs=VMEM,
        compiler_params=pltpu.CompilerParams(vmem_limit_bytes=32 << 20),
    )(mirror, attended, hidden, out_weight, gain)


def solution(mesh):
    fine = Mesh(mesh.devices.reshape((2,) * len(AXES)), AXES)
    spec = P(TM, SENSOR, None)
    return jax.shard_map(
        local,
        mesh=fine,
        in_specs=(spec, P(), P(), P(), P(), P()),
        out_specs=spec,
        check_vma=False,
    )
```
